512 devices in a mesh: dp: 8 (over y, x_hi), expert: 64 (over z, x_lo, core).
Axes of the slice: x: 4 (x_hi: 2, x_lo: 2; x = x_hi * 2 + x_lo), y: 4, z: 16, core: 2. Of those that a mesh axis runs over, the one named last changes fastest.
Arguments:
- tokens: bfloat16 [32768, 2048], P(('dp', 'expert')), parts along dimension 0, may hold values from -6 to 6
- gate_weight: bfloat16 [2048, 16384], P(None, 'expert'), may hold values from -0.125 to 0.125
- up_weight: bfloat16 [2048, 16384], P(None, 'expert'), may hold values from -0.125 to 0.125
- down_weight: bfloat16 [16384, 2048], P('expert'), may hold values from -0.1875 to 0.1875
- route_ids: int32 [32768, 8], P(('dp', 'expert')), parts along dimension 0, may hold values from 0 to 15, all different within a row
- route_weight: float32 [32768, 8], P(('dp', 'expert')), parts along dimension 0, may hold values from 0.2 to 2
Outputs:
- layer_out: bfloat16 [32768, 2048], P(('dp', 'expert')), parts along dimension 0
The draws below stay inside these ranges and needn't reach their ends.
There are 8 independent parts, one for each index of `dp`. The reference program is written for one: setup_inputs(seed, part) draws one part's arguments, and reference() takes and returns one part's arrays. A program takes and returns all parts, laid end to end along the dimension named above; an argument that names none is the same for every part. Nothing has to cross between parts.
Inputs may be any that keep to these rules, and one draw needn't show every extreme that they name: `route_ids`: each token names 8 different experts.
All inputs are finite; a program needn't handle non-finite values.
Results may differ from the reference program's by a relative error of at most 0.0072.
Values may be sent and summed in bfloat16 or wider, within the bound.
A program may use at most 128 MiB of HBM per device.

```python
import math
import jax
import jax.numpy as jnp
from jax import lax

D = 2048
FFW = 1024
EXPERTS = 16
TOP = 8
TOK_DEV = 64
CAP = 32
TOKENS = 4096
HID_DEV = 256
N_EXPERT = 64


def block_scale(own_key, dims, cuts, low, largest):
    loudness = 1.0
    for dim, blocks in cuts:
        draws = jax.random.uniform(jax.random.fold_in(jax.random.fold_in(own_key, 6), dim), (blocks,), jnp.float32, low / len(cuts), largest / len(cuts))
        loudness = loudness * jnp.repeat(jnp.exp(draws), dims[dim] // blocks).reshape((-1,) + (1,) * (len(dims) - 1 - dim))
    return loudness


def distinct(rng, rows, number_of, top, lift):
    sequence = jax.random.permutation(jax.random.fold_in(rng, 1), number_of)
    favour = sequence
    for power in range(3):
        favour = favour * favour // number_of
    favour = favour * lift // number_of
    lots = jax.random.randint(jax.random.fold_in(rng, 2), (rows, number_of), 0, 4096) + favour
    sure = jax.random.permutation(jax.random.fold_in(rng, 3), rows)[jnp.arange(number_of) % rows]
    lots = jnp.where(jnp.arange(rows)[:, None] == sure[None, :], 1 << 14, lots)
    priority = lots * number_of + jnp.arange(number_of)
    return lax.top_k(priority.astype(jnp.int32), top)[1].astype(jnp.int32)


def gaussian(rng, extent, scale, most, split=(), kind=jnp.bfloat16):
    level = block_scale(rng, extent, split, -0.22, 0.18) if split else 1.0
    entries = jax.random.normal(rng, extent, jnp.float32) * scale * level
    return jnp.minimum(jnp.maximum(entries, -most), most).astype(kind)


def setup_inputs(seed: int = 0, part: int = 0) -> dict:
    streams_of = jax.random.split(jax.random.key(seed), 7)
    part_keys = jax.random.split(jax.random.fold_in(streams_of[6], part), 7)
    tokens = gaussian(part_keys[0], (TOKENS, D), 1.0, 6.0, ((0, 64),))
    gate_weight = gaussian(streams_of[1], (D, EXPERTS * FFW), D ** -0.5, 0.125, ((1, 64),))
    up_weight = gaussian(streams_of[2], (D, EXPERTS * FFW), D ** -0.5, 0.125, ((1, 64),))
    down_weight = gaussian(streams_of[3], (EXPERTS * FFW, D), FFW ** -0.5, 0.1875, ((0, 64),))
    route_ids = distinct(part_keys[4], TOKENS, EXPERTS, TOP, 4096)
    route_weight = jnp.clip(jnp.exp(math.log(2.0) - 2.3025851 * jax.random.uniform(part_keys[5], (TOKENS, TOP), jnp.float32) ** block_scale(part_keys[5], (TOKENS, TOP), ((0, 64),), -0.2, 0.2)), 0.2, 2.0)
    return dict(tokens=tokens, gate_weight=gate_weight, up_weight=up_weight, down_weight=down_weight, route_ids=route_ids, route_weight=route_weight)


def tree_sum(parts):
    width = parts.shape[1]
    while width > 1:
        parts = parts.reshape(parts.shape[0], width // 2, 2, parts.shape[-1])
        parts = (parts[:, :, 0].astype(jnp.float32) + parts[:, :, 1].astype(jnp.float32)).astype(jnp.bfloat16)
        parts = lax.optimization_barrier(parts)
        width = width // 2
    return parts[:, 0].astype(jnp.float32)


def reference(tokens, gate_weight, up_weight, down_weight, route_ids, route_weight):
    split_count = N_EXPERT // EXPERTS
    groups = TOKENS // TOK_DEV
    labels = jnp.arange(EXPERTS, dtype=jnp.int32)
    matches = route_ids[:, :, None] == labels[None, None, :]
    counts = jnp.sum(matches.astype(jnp.int32), axis=1)
    raw_shares = jnp.sum(jnp.where(matches, route_weight[:, :, None], jnp.float32(0.0)), axis=1)
    counts_grouped = counts.reshape(groups, TOK_DEV, EXPERTS)
    places = jnp.cumsum(counts_grouped, axis=1) - counts_grouped
    kept_slot = (counts_grouped == 1) & (places < CAP)
    shares = jnp.where(kept_slot.reshape(TOKENS, EXPERTS), raw_shares, jnp.float32(0.0))
    slot_ids = jnp.arange(CAP, dtype=jnp.int32)
    hits = kept_slot[:, :, :, None] & (places[:, :, :, None] == slot_ids[None, None, None, :])
    local_ids = jnp.arange(TOK_DEV, dtype=jnp.int32)
    source = jnp.sum(jnp.where(hits, local_ids[None, :, None, None], jnp.int32(0)), axis=1).astype(jnp.int32)
    filled = jnp.any(hits, axis=1)
    base = (jnp.arange(groups, dtype=jnp.int32) * TOK_DEV).astype(jnp.int32)
    rows_index = (base[:, None, None] + source).astype(jnp.int32)
    picks_all = jnp.transpose(rows_index, (1, 0, 2)).reshape(EXPERTS, groups * CAP)
    live_all = jnp.transpose(filled, (1, 0, 2)).reshape(EXPERTS, groups * CAP)
    shares_t = jnp.transpose(shares)

    def one_expert(running, inputs):
        expert_id, picks, live, share_row = inputs
        first = (expert_id * FFW).astype(jnp.int32)
        gate_part = lax.dynamic_slice_in_dim(gate_weight, first, FFW, 1)
        up_part = lax.dynamic_slice_in_dim(up_weight, first, FFW, 1)
        down_part = lax.dynamic_slice_in_dim(down_weight, first, FFW, 0)
        gathered = jnp.take(tokens, picks, axis=0)
        gathered = jnp.where(live[:, None], gathered, jnp.zeros_like(gathered))
        gate_act = jnp.dot(gathered, gate_part, preferred_element_type=jnp.float32)
        up_act = jnp.dot(gathered, up_part, preferred_element_type=jnp.float32)
        hidden = (jax.nn.silu(gate_act) * up_act).astype(jnp.bfloat16)
        pieces = hidden.reshape(hidden.shape[0], split_count, HID_DEV).astype(jnp.float32)
        down_pieces = down_part.reshape(split_count, HID_DEV, down_part.shape[1]).astype(jnp.float32)
        parts = jnp.einsum("rjh,jhd->rjd", pieces, down_pieces).astype(jnp.bfloat16)
        parts = lax.optimization_barrier(parts)
        expert_out = tree_sum(parts)
        row_weight = jnp.where(live, jnp.take(share_row, picks), jnp.float32(0.0))
        running = running.at[picks].add(row_weight[:, None] * expert_out)
        return running, None

    start_sum = jnp.zeros((tokens.shape[0], tokens.shape[1]), jnp.float32)
    xs = (jnp.arange(EXPERTS, dtype=jnp.int32), picks_all, live_all, shares_t)
    final, unused = lax.scan(one_expert, start_sum, xs)
    return final.astype(jnp.bfloat16)
```

```python
import functools

import jax
import jax.numpy as jnp
from jax import lax
from jax.experimental import pallas as pl
from jax.experimental.pallas import tpu as pltpu
from jax.sharding import PartitionSpec as P

CAP = 32
Q = 16
HALF = 32
MESH = pl.DeviceIdType.MESH


def kernel(nz, tok, gate, up, down, ids, rw, out, tokbuf, rs, contrib, hid, gb, ub, wb, sht, shr, shc,
           ag_send, ag_recv, rs_send, rs_recv, own_sem, sib_send, sib_recv, x_send, x_recv, fw_send, fw_recv,
           sh_send, sh_recv):
    nh = nz // 2
    features = tok.shape[1]
    hdev = gate.shape[1]
    d = lax.axis_index("dp")
    e = lax.axis_index("expert")
    z = e // 4
    core = lax.rem(e, 2)
    x_lo = lax.rem(e // 2, 2)
    x_hi = lax.rem(d, 2)
    n_exp = 4 * nz
    zp = lax.rem(e + 4, n_exp)
    zm = lax.rem(e + n_exp - 4, n_exp)
    sib = e + 1 - 2 * core
    xq = e + 2 - 4 * x_lo
    d_other = d + 1 - 2 * x_hi

    def dev(dd, ee):
        return {"dp": dd, "expert": ee}

    barrier = pltpu.get_barrier_semaphore()
    peers = [(d, sib), (d, xq), (d_other, xq)] + [(d, lax.rem(e + 4 * k, n_exp)) for k in range(1, nz)]
    for dd, ee in peers:
        pl.semaphore_signal(barrier, inc=1, device_id=dev(dd, ee), device_id_type=MESH)
    pl.semaphore_wait(barrier, len(peers))

    def ag_has(dirn, t, q):
        return t < nh or (t == nh and q == dirn)

    def ag_copy(dirn, t, half, q):
        if dirn == 0:
            src_slot, dst_slot, target = t - 1, t, zp
        else:
            src_slot, dst_slot, target = (nz - t + 1) % nz, nz - t, zm
        if t == 1:
            src = tok.at[pl.ds(half * HALF + q * Q, Q), :]
        else:
            src = tokbuf.at[half, pl.ds(src_slot * HALF + q * Q, Q), :]
        i = half * 2 + q
        return pltpu.make_async_remote_copy(
            src_ref=src,
            dst_ref=tokbuf.at[half, pl.ds(dst_slot * HALF + q * Q, Q), :],
            send_sem=ag_send.at[dirn, t - 1, i],
            recv_sem=ag_recv.at[dirn, t - 1, i],
            device_id=dev(d, target),
            device_id_type=MESH,
        )

    def ag_first(half):
        for q in range(2):
            for dirn in range(2):
                if ag_has(dirn, 1, q):
                    ag_copy(dirn, 1, half, q).start()

    def rs_has(dirn, t, q):
        return t > 1 or q == 1 - dirn

    def rs_copy(dirn, t, half, q):
        if dirn == 0:
            src_slot, dst_slot, target = nh - 1 + t, nh + t, zp
        else:
            src_slot, dst_slot, target = nh + 1 - t, nh - t, zm
        i = half * 2 + q
        return pltpu.make_async_remote_copy(
            src_ref=rs.at[half, src_slot, pl.ds(q * Q, Q), :],
            dst_ref=rs.at[half, dst_slot, pl.ds(q * Q, Q), :],
            send_sem=rs_send.at[dirn, t - 1, i],
            recv_sem=rs_recv.at[dirn, t - 1, i],
            device_id=dev(d, target),
            device_id_type=MESH,
        )

    def rs_hop(dirn, t, half, q):
        if not rs_has(dirn, t, q):
            return
        slot = nh - 1 + t if dirn == 0 else nh + 1 - t
        rows = pl.ds(q * Q, Q)
        total = contrib[half, pl.ds(slot * HALF + q * Q, Q), :]
        if t > 1 and rs_has(dirn, t - 1, q):
            rs_copy(dirn, t - 1, half, q).wait_recv()
            total = total + rs[half, slot, rows, :].astype(jnp.float32)
        rs[half, slot, rows, :] = total.astype(jnp.bfloat16)
        rs_copy(dirn, t, half, q).start()

    def rs_last(half, q):
        rows = pl.ds(q * Q, Q)
        rs_copy(0, nh, half, q).wait_recv()
        rs_copy(1, nh, half, q).wait_recv()
        total = contrib[half, pl.ds(q * Q, Q), :]
        total = total + rs[half, 0, rows, :].astype(jnp.float32) + rs[half, nz, rows, :].astype(jnp.float32)
        out[pl.ds(half * HALF + q * Q, Q), :] = total.astype(jnp.bfloat16)

    sources = (gate, up, down)

    def whole(i, role):
        if i == 2:
            return wb.at[pl.ds(role * hdev, hdev), :]
        return (gb, ub)[i].at[role]

    def part(i, role, side):
        if i == 2:
            return wb.at[pl.ds(role * hdev + side * (hdev // 2), hdev // 2), :]
        return (gb, ub)[i].at[role, pl.ds(side * (features // 2), features // 2), :]

    def own_copy(i):
        return pltpu.make_async_copy(sources[i], whole(i, 0), own_sem.at[i])

    def sib_copy(i):
        return pltpu.make_async_remote_copy(
            src_ref=sources[i], dst_ref=whole(i, 1), send_sem=sib_send.at[i], recv_sem=sib_recv.at[i],
            device_id=dev(d, sib), device_id_type=MESH)

    def x_copy(i, side):
        size = sources[i].shape[0] // 2
        return pltpu.make_async_remote_copy(
            src_ref=sources[i].at[pl.ds(side * size, size), :], dst_ref=part(i, 2, side),
            send_sem=x_send.at[i, side], recv_sem=x_recv.at[i, side],
            device_id=dev(d if side == 0 else d_other, xq), device_id_type=MESH)

    def fw_copy(i, side):
        return pltpu.make_async_remote_copy(
            src_ref=part(i, 2, side), dst_ref=part(i, 3, side),
            send_sem=fw_send.at[i, side], recv_sem=fw_recv.at[i, side],
            device_id=dev(d, sib), device_id_type=MESH)

    def forward(i):
        for side in range(2):
            x_copy(i, side).wait_recv()
            fw_copy(i, side).start()

    def arrive(i, role):
        if role == 0:
            own_copy(i).wait()
        elif role == 1:
            sib_copy(i).wait_recv()
        elif role == 3:
            for side in range(2):
                fw_copy(i, side).wait_recv()

    def share_copy(k):
        there = lax.rem(z + k, nz)
        return pltpu.make_async_remote_copy(
            src_ref=sht.at[there], dst_ref=shr.at[k], send_sem=sh_send.at[k], recv_sem=sh_recv.at[k],
            device_id=dev(d, lax.rem(e + 4 * k, n_exp)), device_id_type=MESH)

    def make_shares():
        lane = lax.broadcasted_iota(jnp.int32, (64, 128), 1)
        counts = jnp.zeros((64, 128), jnp.float32)
        raw = jnp.zeros((64, 128), jnp.float32)
        for k in range(ids.shape[1]):
            match = ids[:, k:k + 1] == lane
            counts = counts + jnp.where(match, 1.0, 0.0)
            raw = raw + jnp.where(match, rw[:, k:k + 1], 0.0)
        before = lax.broadcasted_iota(jnp.int32, (64, 64), 1) < lax.broadcasted_iota(jnp.int32, (64, 64), 0)
        places = jnp.dot(jnp.where(before, 1.0, 0.0).astype(jnp.bfloat16), counts.astype(jnp.bfloat16),
                         preferred_element_type=jnp.float32)
        shares = jnp.where((counts == 1.0) & (places < CAP), raw, 0.0)
        turned = jnp.concatenate([shares, jnp.zeros((64, 128), jnp.float32)], axis=0).T
        for i in range(nz):
            sht[i, :, :] = turned[i:i + 1, :]
        for k in range(1, nz):
            share_copy(k).start()

    def take_shares():
        diag = lax.broadcasted_iota(jnp.int32, (64, 128), 1) == lax.broadcasted_iota(jnp.int32, (64, 128), 0)
        for k in range(nz):
            if k == 0:
                row = sht[z]
            else:
                share_copy(k).wait_recv()
                row = shr[k]
            column = jnp.sum(jnp.where(diag, row, 0.0), axis=1, keepdims=True)
            shc[0, pl.ds(k * HALF, HALF), :] = column[:HALF]
            shc[1, pl.ds(k * HALF, HALF), :] = column[HALF:]

    def hidden(half, role):
        tile = min(256, nz * HALF)

        def body(m, carry):
            rows = pl.ds(pl.multiple_of(m * tile, tile), tile)
            x = tokbuf[half, rows, :]
            g = jnp.dot(x, gb[role], preferred_element_type=jnp.float32)
            v = jnp.dot(x, ub[role], preferred_element_type=jnp.float32)
            hid[rows, role * hdev:(role + 1) * hdev] = (g / (1.0 + jnp.exp(-g)) * v).astype(jnp.bfloat16)
            return carry

        lax.fori_loop(0, nz * HALF // tile, body, 0)

    def project(half, n):
        tile = min(256, nz * HALF)
        width = features // 4

        def body(m, carry):
            rows = pl.ds(pl.multiple_of(m * tile, tile), tile)
            cols = slice(n * width, (n + 1) * width)
            acc = jnp.dot(hid[rows, :], wb[:, cols], preferred_element_type=jnp.float32)
            contrib[half, rows, cols] = acc * shc[half, rows, :]
            return carry

        lax.fori_loop(0, nz * HALF // tile, body, 0)

    ag_first(0)
    for i in range(3):
        for side in range(2):
            x_copy(i, side).start()
    for i in range(3):
        sib_copy(i).start()
        own_copy(i).start()
    for half in range(2):
        pltpu.make_async_copy(tok.at[pl.ds(half * HALF, HALF), :], tokbuf.at[half, pl.ds(0, HALF), :],
                              own_sem.at[3 + half]).start()
    make_shares()

    def spread(half, t):
        for q in range(2):
            for dirn in range(2):
                if ag_has(dirn, t, q):
                    ag_copy(dirn, t, half, q).wait_recv()
                if t < nh and ag_has(dirn, t + 1, q):
                    ag_copy(dirn, t + 1, half, q).start()

    for t in range(1, nh + 1):
        spread(0, t)
        if t == max(1, nh - 2):
            ag_first(1)
        if t == max(1, nh - 2):
            forward(0)
    for half in range(2):
        pltpu.make_async_copy(tok.at[pl.ds(half * HALF, HALF), :], tokbuf.at[half, pl.ds(0, HALF), :],
                              own_sem.at[3 + half]).wait()

    def work(half, t):
        step = (t - 1) * 8 // nh
        steps = max(1, 8 // nh)
        for s in range(step, step + steps):
            if s < 4:
                if half == 0:
                    arrive(0, s)
                    arrive(1, s)
                hidden(half, s)
            else:
                if half == 0 and s == 4:
                    take_shares()
                    forward(2)
                    for role in range(4):
                        arrive(2, role)
                project(half, s - 4)
            if half == 0 and s == 1:
                forward(1)

    for t in range(1, nh + 1):
        spread(1, t)
        work(0, t)

    for t in range(1, nh + 1):
        for q in range(2):
            for dirn in range(2):
                rs_hop(dirn, t, 0, q)
        work(1, t)
    for t in range(1, nh + 1):
        for q in range(2):
            for dirn in range(2):
                rs_hop(dirn, t, 1, q)
        if t == 2:
            rs_last(0, 0)
            rs_last(0, 1)
        if t == 3:
            for half in range(2):
                for tt in range(1, nh + 1):
                    for q in range(2):
                        for dirn in range(2):
                            if ag_has(dirn, tt, q):
                                ag_copy(dirn, tt, half, q).wait_send()
        if t == 4:
            for i in range(3):
                sib_copy(i).wait_send()
                for side in range(2):
                    x_copy(i, side).wait_send()
                    fw_copy(i, side).wait_send()
            for k in range(1, nz):
                share_copy(k).wait_send()
    for q in range(2):
        rs_last(1, q)
    for half in range(2):
        for t in range(1, nh + 1):
            for q in range(2):
                for dirn in range(2):
                    if rs_has(dirn, t, q):
                        rs_copy(dirn, t, half, q).wait_send()


def solution(mesh):
    nz = mesh.shape["expert"] // 4
    nh = nz // 2

    def on_device(tokens, gate, up, down, ids, rw):
        rows, features = tokens.shape
        hdev = gate.shape[1]
        dma = pltpu.SemaphoreType.DMA
        flops = 2 * rows * nz * features * 4 * hdev * 3
        return pl.pallas_call(
            functools.partial(kernel, nz),
            out_shape=jax.ShapeDtypeStruct((rows, features), jnp.bfloat16),
            in_specs=[pl.BlockSpec(memory_space=pl.ANY)] * 4 + [pl.BlockSpec(memory_space=pltpu.VMEM)] * 2,
            out_specs=pl.BlockSpec(memory_space=pltpu.VMEM),
            scratch_shapes=[
                pltpu.VMEM((2, nz * HALF, features), jnp.bfloat16),
                pltpu.VMEM((2, nz + 1, HALF, features), jnp.bfloat16),
                pltpu.VMEM((2, nz * HALF, features), jnp.float32),
                pltpu.VMEM((nz * HALF, 4 * hdev), jnp.bfloat16),
                pltpu.VMEM((4, features, hdev), jnp.bfloat16),
                pltpu.VMEM((4, features, hdev), jnp.bfloat16),
                pltpu.VMEM((4 * hdev, features), jnp.bfloat16),
                pltpu.VMEM((nz, 1, 128), jnp.float32),
                pltpu.VMEM((nz, 1, 128), jnp.float32),
                pltpu.VMEM((2, nz * HALF, 1), jnp.float32),
                dma((2, nh, 4)),
                dma((2, nh, 4)),
                dma((2, nh, 4)),
                dma((2, nh, 4)),
                dma((5,)),
                dma((3,)),
                dma((3,)),
                dma((3, 2)),
                dma((3, 2)),
                dma((3, 2)),
                dma((3, 2)),
                dma((nz,)),
                dma((nz,)),
            ],
            compiler_params=pltpu.CompilerParams(
                collective_id=0, has_side_effects=True, vmem_limit_bytes=56 * 1024 * 1024
            ),
            cost_estimate=pl.CostEstimate(flops=flops, bytes_accessed=4 * 1024 * 1024, transcendentals=0),
        )(tokens, gate, up, down, ids, rw)

    return jax.shard_map(
        on_device,
        mesh=mesh,
        in_specs=(
            P(("dp", "expert"), None),
            P(None, "expert"),
            P(None, "expert"),
            P("expert", None),
            P(("dp", "expert"), None),
            P(("dp", "expert"), None),
        ),
        out_specs=P(("dp", "expert"), None),
        check_vma=False,
    )
```

```python
import functools

import jax
import jax.numpy as jnp
from jax import lax
from jax.experimental import pallas as pl
from jax.experimental.pallas import tpu as pltpu
from jax.sharding import PartitionSpec as P

CAP = 32
Q = 16
HALF = 32
MESH = pl.DeviceIdType.MESH


def kernel(nz, tok, gate, up, down, ids, rw, out, tokbuf, rs, contrib, hid, gb, ub, wb, shr, shc,
           ag_send, ag_recv, rs_send, rs_recv, own_sem, sib_send, sib_recv, x_send, x_recv, fw_send, fw_recv,
           sh_send, sh_recv):
    nh = nz // 2
    order = [0] + [s for t in range(1, nh) for s in (t, nz - t)] + [nh]
    place = {slot: i * HALF for i, slot in enumerate(order)}
    features = tok.shape[1]
    hdev = gate.shape[1]
    d = lax.axis_index("dp")
    e = lax.axis_index("expert")
    z = e // 4
    core = lax.rem(e, 2)
    x_lo = lax.rem(e // 2, 2)
    x_hi = lax.rem(d, 2)
    n_exp = 4 * nz
    zp = lax.rem(e + 4, n_exp)
    zm = lax.rem(e + n_exp - 4, n_exp)
    sib = e + 1 - 2 * core
    xq = e + 2 - 4 * x_lo
    d_other = d + 1 - 2 * x_hi

    def dev(dd, ee):
        return {"dp": dd, "expert": ee}

    barrier = pltpu.get_barrier_semaphore()
    peers = [(d, zp), (d, zm), (d, xq), (d_other, xq), (d, sib)]
    for dd, ee in peers:
        pl.semaphore_signal(barrier, inc=1, device_id=dev(dd, ee), device_id_type=MESH)

    def ag_has(dirn, t, q):
        return t < nh or (t == nh and q == dirn)

    def ag_copy(dirn, t, half, q):
        if dirn == 0:
            src_slot, dst_slot, target = t - 1, t, zp
        else:
            src_slot, dst_slot, target = (nz - t + 1) % nz, nz - t, zm
        if t == 1:
            src = tok.at[pl.ds(half * HALF + q * Q, Q), :]
        else:
            src = tokbuf.at[half, pl.ds(place[src_slot] + q * Q, Q), :]
        i = half * 2 + q
        return pltpu.make_async_remote_copy(
            src_ref=src,
            dst_ref=tokbuf.at[half, pl.ds(place[dst_slot] + q * Q, Q), :],
            send_sem=ag_send.at[dirn, t - 1, i],
            recv_sem=ag_recv.at[dirn, t - 1, i],
            device_id=dev(d, target),
            device_id_type=MESH,
        )

    def ag_first(half):
        for q in range(2):
            for dirn in range(2):
                if ag_has(dirn, 1, q):
                    ag_copy(dirn, 1, half, q).start()

    def rs_has(dirn, t, q):
        return t > 1 or q == 1 - dirn

    def rs_copy(dirn, t, half, q):
        if dirn == 0:
            src_slot, dst_slot, target = nh - 1 + t, nh + t, zp
        else:
            src_slot, dst_slot, target = nh + 1 - t, nh - t, zm
        i = half * 2 + q
        return pltpu.make_async_remote_copy(
            src_ref=rs.at[half, src_slot, pl.ds(q * Q, Q), :],
            dst_ref=rs.at[half, dst_slot, pl.ds(q * Q, Q), :],
            send_sem=rs_send.at[dirn, t - 1, i],
            recv_sem=rs_recv.at[dirn, t - 1, i],
            device_id=dev(d, target),
            device_id_type=MESH,
        )

    def rs_hop(dirn, t, half, q):
        if not rs_has(dirn, t, q):
            return
        slot = nh - 1 + t if dirn == 0 else nh + 1 - t
        rows = pl.ds(q * Q, Q)
        total = contrib[half, pl.ds(place[slot] + q * Q, Q), :]
        if t > 1 and rs_has(dirn, t - 1, q):
            rs_copy(dirn, t - 1, half, q).wait_recv()
            total = total + rs[half, slot, rows, :].astype(jnp.float32)
        rs[half, slot, rows, :] = total.astype(jnp.bfloat16)
        rs_copy(dirn, t, half, q).start()

    def rs_last(half, q):
        rows = pl.ds(q * Q, Q)
        rs_copy(0, nh, half, q).wait_recv()
        rs_copy(1, nh, half, q).wait_recv()
        total = contrib[half, pl.ds(q * Q, Q), :]
        total = total + rs[half, 0, rows, :].astype(jnp.float32) + rs[half, nz, rows, :].astype(jnp.float32)
        out[pl.ds(half * HALF + q * Q, Q), :] = total.astype(jnp.bfloat16)

    sources = (gate, up, down)

    def whole(i, role):
        if i == 2:
            return wb.at[pl.ds(role * hdev, hdev), :]
        return (gb, ub)[i].at[role]

    def part(i, role, side):
        if i == 2:
            return wb.at[pl.ds(role * hdev + side * (hdev // 2), hdev // 2), :]
        return (gb, ub)[i].at[role, pl.ds(side * (features // 2), features // 2), :]

    def own_copy(i):
        return pltpu.make_async_copy(sources[i], whole(i, 0), own_sem.at[i])

    def sib_copy(i):
        return pltpu.make_async_remote_copy(
            src_ref=sources[i], dst_ref=whole(i, 1), send_sem=sib_send.at[i], recv_sem=sib_recv.at[i],
            device_id=dev(d, sib), device_id_type=MESH)

    def x_copy(i, side):
        size = sources[i].shape[0] // 2
        return pltpu.make_async_remote_copy(
            src_ref=sources[i].at[pl.ds(side * size, size), :], dst_ref=part(i, 2, side),
            send_sem=x_send.at[i, side], recv_sem=x_recv.at[i, side],
            device_id=dev(d if side == 0 else d_other, xq), device_id_type=MESH)

    def fw_copy(i, side):
        return pltpu.make_async_remote_copy(
            src_ref=part(i, 2, side), dst_ref=part(i, 3, side),
            send_sem=fw_send.at[i, side], recv_sem=fw_recv.at[i, side],
            device_id=dev(d, sib), device_id_type=MESH)

    def forward(i):
        for side in range(2):
            x_copy(i, side).wait_recv()
            fw_copy(i, side).start()

    def arrive(i, role):
        if role == 0:
            own_copy(i).wait()
        elif role == 1:
            sib_copy(i).wait_recv()
        elif role == 3:
            for side in range(2):
                fw_copy(i, side).wait_recv()

    def share_has(dirn, t):
        return t < nh or dirn == 0

    def share_copy(dirn, t):
        if dirn == 0:
            src_slot, dst_slot, target = t - 1, t, zp
        else:
            src_slot, dst_slot, target = (nz - t + 1) % nz, nz - t, zm
        return pltpu.make_async_remote_copy(
            src_ref=shr.at[src_slot], dst_ref=shr.at[dst_slot],
            send_sem=sh_send.at[dirn, t - 1], recv_sem=sh_recv.at[dirn, t - 1],
            device_id=dev(d, target), device_id_type=MESH)

    def make_shares():
        experts = lax.broadcasted_iota(jnp.int32, (nz, 64), 0)
        counts = jnp.zeros((nz, 64), jnp.float32)
        raw = jnp.zeros((nz, 64), jnp.float32)
        for k in range(ids.shape[0]):
            match = ids[k:k + 1, :] == experts
            counts = counts + jnp.where(match, 1.0, 0.0)
            raw = raw + jnp.where(match, rw[k:k + 1, :], 0.0)
        before = lax.broadcasted_iota(jnp.int32, (64, 64), 0) < lax.broadcasted_iota(jnp.int32, (64, 64), 1)
        places = jnp.dot(counts.astype(jnp.bfloat16), jnp.where(before, 1.0, 0.0).astype(jnp.bfloat16),
                         preferred_element_type=jnp.float32)
        shares = jnp.where((counts == 1.0) & (places < CAP), raw, 0.0)
        for k in range(nz // 8):
            shr[0, :, k * 64:(k + 1) * 64] = shares[k * 8:(k + 1) * 8, :]

    def take_shares(slots):
        lane = lax.broadcasted_iota(jnp.int32, (64, 128), 1)
        row = lax.broadcasted_iota(jnp.int32, (64, 128), 0)
        diag = lane == row + 64 * (z // 8)
        for slot in slots:
            mine = shr[slot, pl.ds(lax.rem(z, 8), 1), :]
            column = jnp.sum(jnp.where(diag, mine, 0.0), axis=1, keepdims=True)
            shc[0, pl.ds(place[slot], HALF), :] = column[:HALF]
            shc[1, pl.ds(place[slot], HALF), :] = column[HALF:]

    tile = nz * HALF // 2

    def hidden(half, m, role):
        rows = pl.ds(m * tile, tile)
        x = tokbuf[half, rows, :]
        g = jnp.dot(x, gb[role], preferred_element_type=jnp.float32)
        v = jnp.dot(x, ub[role], preferred_element_type=jnp.float32)
        hid[half, rows, role * hdev:(role + 1) * hdev] = (g / (1.0 + jnp.exp(-g)) * v).astype(jnp.bfloat16)

    def project(half, m, n):
        rows = pl.ds(m * tile, tile)
        width = features // 4
        cols = slice(n * width, (n + 1) * width)
        acc = jnp.dot(hid[half, rows, :], wb[:, cols], preferred_element_type=jnp.float32)
        contrib[half, rows, cols] = acc * shc[half, rows, :]

    for i in range(3):
        own_copy(i).start()
    for half in range(2):
        pltpu.make_async_copy(tok.at[pl.ds(half * HALF, HALF), :], tokbuf.at[half, pl.ds(0, HALF), :],
                              own_sem.at[3 + half]).start()
    make_shares()
    pl.semaphore_wait(barrier, len(peers))

    ag_first(0)
    for dirn in range(2):
        share_copy(dirn, 1).start()
    ag_first(1)
    for i in range(2):
        for side in range(2):
            x_copy(i, side).start()
    for i in range(3):
        sib_copy(i).start()

    def spread(half, t):
        for q in range(2):
            for dirn in range(2):
                if ag_has(dirn, t, q):
                    ag_copy(dirn, t, half, q).wait_recv()
                if t < nh and ag_has(dirn, t + 1, q):
                    ag_copy(dirn, t + 1, half, q).start()

    def spread_shares(t):
        for dirn in range(2):
            if share_has(dirn, t):
                share_copy(dirn, t).wait_recv()
            if t < nh and share_has(dirn, t + 1):
                share_copy(dirn, t + 1).start()

    for t in range(1, nh + 1):
        spread(0, t)
        spread_shares(t)
        if t < nh:
            spread(1, t)
        if t == 2:
            for side in range(2):
                x_copy(2, side).start()
        if t == 4:
            for half in range(2):
                pltpu.make_async_copy(tok.at[pl.ds(half * HALF, HALF), :], tokbuf.at[half, pl.ds(0, HALF), :],
                                      own_sem.at[3 + half]).wait()
            for role in range(2):
                arrive(0, role)
                arrive(1, role)
                for half in range(2):
                    hidden(half, 0, role)
        if t == 5:
            forward(0)
            forward(1)
            for half in range(2):
                hidden(half, 0, 2)
        if t == 6:
            arrive(0, 3)
            arrive(1, 3)
            for half in range(2):
                hidden(half, 0, 3)
            take_shares(order[:nz // 2])
        if t == 7:
            forward(2)
            for role in range(4):
                arrive(2, role)
            for half in range(2):
                for n in range(4):
                    project(half, 0, n)

    def last_tile(half):
        for role in range(4):
            hidden(half, 1, role)
        if half == 0:
            take_shares(order[nz // 2:])
        for n in range(4):
            project(half, 1, n)

    def back(half, t):
        for q in range(2):
            for dirn in range(2):
                if t == 1 or rs_has(dirn, 1, q):
                    rs_hop(dirn, t if rs_has(dirn, t, q) else t + 1, half, q)
                elif t > 2:
                    rs_hop(dirn, t, half, q)

    last_tile(0)
    back(0, 1)
    spread(1, nh)
    last_tile(1)
    back(1, 1)
    for t in range(2, nh + 1):
        for half in range(2):
            back(half, t)
        if t == 3:
            for half in range(2):
                for tt in range(1, nh + 1):
                    for q in range(2):
                        for dirn in range(2):
                            if ag_has(dirn, tt, q):
                                ag_copy(dirn, tt, half, q).wait_send()
        if t == 4:
            for i in range(3):
                sib_copy(i).wait_send()
                for side in range(2):
                    x_copy(i, side).wait_send()
                    fw_copy(i, side).wait_send()
            for tt in range(1, nh + 1):
                for dirn in range(2):
                    if share_has(dirn, tt):
                        share_copy(dirn, tt).wait_send()
    for half in range(2):
        for q in range(2):
            rs_last(half, q)
    for half in range(2):
        for t in range(1, nh + 1):
            for q in range(2):
                for dirn in range(2):
                    if rs_has(dirn, t, q):
                        rs_copy(dirn, t, half, q).wait_send()


def solution(mesh):
    nz = mesh.shape["expert"] // 4
    nh = nz // 2

    def on_device(tokens, gate, up, down, ids, rw):
        rows, features = tokens.shape
        hdev = gate.shape[1]
        dma = pltpu.SemaphoreType.DMA
        flops = 2 * rows * nz * features * 4 * hdev * 3
        return pl.pallas_call(
            functools.partial(kernel, nz),
            out_shape=jax.ShapeDtypeStruct((rows, features), jnp.bfloat16),
            in_specs=[pl.BlockSpec(memory_space=pl.ANY)] * 4 + [pl.BlockSpec(memory_space=pltpu.VMEM)] * 2,
            out_specs=pl.BlockSpec(memory_space=pltpu.VMEM),
            scratch_shapes=[
                pltpu.VMEM((2, nz * HALF, features), jnp.bfloat16),
                pltpu.VMEM((2, nz + 1, HALF, features), jnp.bfloat16),
                pltpu.VMEM((2, nz * HALF, features), jnp.float32),
                pltpu.VMEM((2, nz * HALF, 4 * hdev), jnp.bfloat16),
                pltpu.VMEM((4, features, hdev), jnp.bfloat16),
                pltpu.VMEM((4, features, hdev), jnp.bfloat16),
                pltpu.VMEM((4 * hdev, features), jnp.bfloat16),
                pltpu.VMEM((nz, 8, 128), jnp.float32),
                pltpu.VMEM((2, nz * HALF, 1), jnp.float32),
                dma((2, nh, 4)),
                dma((2, nh, 4)),
                dma((2, nh, 4)),
                dma((2, nh, 4)),
                dma((5,)),
                dma((3,)),
                dma((3,)),
                dma((3, 2)),
                dma((3, 2)),
                dma((3, 2)),
                dma((3, 2)),
                dma((2, nh)),
                dma((2, nh)),
            ],
            compiler_params=pltpu.CompilerParams(
                collective_id=0, has_side_effects=True, vmem_limit_bytes=56 * 1024 * 1024
            ),
            cost_estimate=pl.CostEstimate(flops=flops, bytes_accessed=4 * 1024 * 1024, transcendentals=0),
        )(tokens, gate, up, down, ids.T, rw.T)

    return jax.shard_map(
        on_device,
        mesh=mesh,
        in_specs=(
            P(("dp", "expert"), None),
            P(None, "expert"),
            P(None, "expert"),
            P("expert", None),
            P(("dp", "expert"), None),
            P(("dp", "expert"), None),
        ),
        out_specs=P(("dp", "expert"), None),
        check_vma=False,
    )
```

```python
import functools

import jax
import jax.numpy as jnp
from jax import lax
from jax.experimental import pallas as pl
from jax.experimental.pallas import tpu as pltpu
from jax.sharding import PartitionSpec as P

CAP = 32
Q = 16
HALF = 32
MESH = pl.DeviceIdType.MESH


def kernel(nz, tok, gate, up, down, ids_hbm, rw_hbm, out, tokbuf, rs, contrib, hid, gb, ub, wb, shr, shc, ids, rw, outbuf,
           ag_send, ag_recv, rs_send, rs_recv, own_sem, sib_send, sib_recv, x_send, x_recv, fw_send, fw_recv,
           sh_send, sh_recv, in_sem, out_sem):
    nh = nz // 2
    order = [0] + [s for t in range(1, nh) for s in (t, nz - t)] + [nh]
    early, middle, late, last = order[:nh], order[nh:nh + nh // 2], order[nh + nh // 2:-1], order[-1:]
    place, tiles, row = {}, {}, 0
    for name, slots, halves in (("A0", early, (0,)), ("A1", early, (1,)), ("B", middle, (0, 1)), ("C", late, (0, 1)), ("D", last, (0, 1))):
        tiles[name] = (row, len(slots) * len(halves) * HALF)
        for half in halves:
            for slot in slots:
                place[half, slot] = row
                row += HALF
    features = tok.shape[1]
    hdev = gate.shape[1]
    d = lax.axis_index("dp")
    e = lax.axis_index("expert")
    z = e // 4
    core = lax.rem(e, 2)
    x_lo = lax.rem(e // 2, 2)
    x_hi = lax.rem(d, 2)
    n_exp = 4 * nz
    zp = lax.rem(e + 4, n_exp)
    zm = lax.rem(e + n_exp - 4, n_exp)
    sib = e + 1 - 2 * core
    xq = e + 2 - 4 * x_lo
    d_other = d + 1 - 2 * x_hi

    def dev(dd, ee):
        return {"dp": dd, "expert": ee}

    barrier = pltpu.get_barrier_semaphore()
    peers = [(d, zp), (d, zm), (d, xq), (d_other, xq), (d, sib)]
    for dd, ee in peers:
        pl.semaphore_signal(barrier, inc=1, device_id=dev(dd, ee), device_id_type=MESH)

    def ag_has(dirn, t, q):
        return t < nh or (t == nh and q == dirn)

    def ag_copy(dirn, t, half, q):
        if dirn == 0:
            src_slot, dst_slot, target = t - 1, t, zp
        else:
            src_slot, dst_slot, target = (nz - t + 1) % nz, nz - t, zm
        if t == 1:
            src = tok.at[pl.ds(half * HALF + q * Q, Q), :]
        else:
            src = tokbuf.at[pl.ds(place[half, src_slot] + q * Q, Q), :]
        i = half * 2 + q
        return pltpu.make_async_remote_copy(
            src_ref=src,
            dst_ref=tokbuf.at[pl.ds(place[half, dst_slot] + q * Q, Q), :],
            send_sem=ag_send.at[dirn, t - 1, i],
            recv_sem=ag_recv.at[dirn, t - 1, i],
            device_id=dev(d, target),
            device_id_type=MESH,
        )

    def ag_first(half):
        for q in range(2):
            for dirn in range(2):
                if ag_has(dirn, 1, q):
                    ag_copy(dirn, 1, half, q).start()

    def rs_has(dirn, t, q):
        return t > 1 or q == 1 - dirn

    def rs_copy(dirn, t, half, q):
        if dirn == 0:
            src_slot, dst_slot, target = nh - 1 + t, nh + t, zp
        else:
            src_slot, dst_slot, target = nh + 1 - t, nh - t, zm
        i = half * 2 + q
        return pltpu.make_async_remote_copy(
            src_ref=rs.at[half, src_slot, pl.ds(q * Q, Q), :],
            dst_ref=rs.at[half, dst_slot, pl.ds(q * Q, Q), :],
            send_sem=rs_send.at[dirn, t - 1, i],
            recv_sem=rs_recv.at[dirn, t - 1, i],
            device_id=dev(d, target),
            device_id_type=MESH,
        )

    def rs_hop(dirn, t, half, q):
        if not rs_has(dirn, t, q):
            return
        slot = nh - 1 + t if dirn == 0 else nh + 1 - t
        rows = pl.ds(q * Q, Q)
        total = contrib[pl.ds(place[half, slot] + q * Q, Q), :]
        if t > 1 and rs_has(dirn, t - 1, q):
            rs_copy(dirn, t - 1, half, q).wait_recv()
            total = total + rs[half, slot, rows, :].astype(jnp.float32)
        rs[half, slot, rows, :] = total.astype(jnp.bfloat16)
        rs_copy(dirn, t, half, q).start()

    def rs_last(half, q):
        rows = pl.ds(q * Q, Q)
        rs_copy(0, nh, half, q).wait_recv()
        rs_copy(1, nh, half, q).wait_recv()
        total = contrib[pl.ds(place[half, 0] + q * Q, Q), :]
        total = total + rs[half, 0, rows, :].astype(jnp.float32) + rs[half, nz, rows, :].astype(jnp.float32)
        outbuf[pl.ds(half * HALF + q * Q, Q), :] = total.astype(jnp.bfloat16)
        out_copy(half, q).start()

    def out_copy(half, q):
        rows = pl.ds(half * HALF + q * Q, Q)
        return pltpu.make_async_copy(outbuf.at[rows, :], out.at[rows, :], out_sem.at[half * 2 + q])

    sources = (gate, up, down)

    def whole(i, role):
        if i == 2:
            return wb.at[pl.ds(role * hdev, hdev), :]
        return (gb, ub)[i].at[role]

    def part(i, role, side):
        if i == 2:
            return wb.at[pl.ds(role * hdev + side * (hdev // 2), hdev // 2), :]
        return (gb, ub)[i].at[role, pl.ds(side * (features // 2), features // 2), :]

    def own_copy(i):
        return pltpu.make_async_copy(sources[i], whole(i, 0), own_sem.at[i])

    def piece(i, role, k):
        size = sources[i].shape[0] // 4
        if i == 2:
            return wb.at[pl.ds(role * hdev + k * size, size), :]
        return (gb, ub)[i].at[role, pl.ds(k * size, size), :]

    def sib_copy(i, k):
        size = sources[i].shape[0] // 4
        return pltpu.make_async_remote_copy(
            src_ref=sources[i].at[pl.ds(k * size, size), :], dst_ref=piece(i, 1, k),
            send_sem=sib_send.at[i, k], recv_sem=sib_recv.at[i, k],
            device_id=dev(d, sib), device_id_type=MESH)

    def x_copy(i, side):
        size = sources[i].shape[0] // 2
        return pltpu.make_async_remote_copy(
            src_ref=sources[i].at[pl.ds(side * size, size), :], dst_ref=part(i, 2, side),
            send_sem=x_send.at[i, side], recv_sem=x_recv.at[i, side],
            device_id=dev(d if side == 0 else d_other, xq), device_id_type=MESH)

    def fw_copy(i, k):
        return pltpu.make_async_remote_copy(
            src_ref=piece(i, 2, k), dst_ref=piece(i, 3, k),
            send_sem=fw_send.at[i, k], recv_sem=fw_recv.at[i, k],
            device_id=dev(d, sib), device_id_type=MESH)

    def forward(i, side):
        x_copy(i, side).wait_recv()
        for k in range(2):
            fw_copy(i, side * 2 + k).start()

    def arrive(i, role):
        if role == 0:
            own_copy(i).wait()
        for k in range(4):
            if role == 1:
                sib_copy(i, k).wait_recv()
            elif role == 3:
                fw_copy(i, k).wait_recv()

    def share_has(dirn, t):
        return t < nh or dirn == 0

    def share_copy(dirn, t):
        if dirn == 0:
            src_slot, dst_slot, target = t - 1, t, zp
        else:
            src_slot, dst_slot, target = (nz - t + 1) % nz, nz - t, zm
        return pltpu.make_async_remote_copy(
            src_ref=shr.at[src_slot], dst_ref=shr.at[dst_slot],
            send_sem=sh_send.at[dirn, t - 1], recv_sem=sh_recv.at[dirn, t - 1],
            device_id=dev(d, target), device_id_type=MESH)

    def make_shares():
        experts = lax.broadcasted_iota(jnp.int32, (nz, 64), 0)
        counts = jnp.zeros((nz, 64), jnp.float32)
        raw = jnp.zeros((nz, 64), jnp.float32)
        for k in range(ids.shape[0]):
            match = ids[k:k + 1, :] == experts
            counts = counts + jnp.where(match, 1.0, 0.0)
            raw = raw + jnp.where(match, rw[k:k + 1, :], 0.0)
        before = lax.broadcasted_iota(jnp.int32, (64, 64), 0) < lax.broadcasted_iota(jnp.int32, (64, 64), 1)
        places = jnp.dot(counts.astype(jnp.bfloat16), jnp.where(before, 1.0, 0.0).astype(jnp.bfloat16),
                         preferred_element_type=jnp.float32)
        shares = jnp.where((counts == 1.0) & (places < CAP), raw, 0.0)
        for k in range(nz // 8):
            shr[0, :, k * 64:(k + 1) * 64] = shares[k * 8:(k + 1) * 8, :]

    def take_shares(slots):
        lane = lax.broadcasted_iota(jnp.int32, (64, 128), 1)
        row = lax.broadcasted_iota(jnp.int32, (64, 128), 0)
        diag = lane == row + 64 * (z // 8)
        for slot in slots:
            mine = shr[slot, pl.ds(lax.rem(z, 8), 1), :]
            column = jnp.sum(jnp.where(diag, mine, 0.0), axis=1, keepdims=True)
            for half in range(2):
                shc[pl.ds(place[half, slot], HALF), :] = column[half * HALF:(half + 1) * HALF]

    def hidden(m, role):
        rows = pl.ds(*tiles[m])
        x = tokbuf[rows, :]
        g = jnp.dot(x, gb[role], preferred_element_type=jnp.float32)
        v = jnp.dot(x, ub[role], preferred_element_type=jnp.float32)
        hid[rows, role * hdev:(role + 1) * hdev] = (g / (1.0 + jnp.exp(-g)) * v).astype(jnp.bfloat16)

    def project(m, n):
        rows = pl.ds(*tiles[m])
        width = features // 4
        cols = slice(n * width, (n + 1) * width)
        acc = jnp.dot(hid[rows, :], wb[:, cols], preferred_element_type=jnp.float32)
        contrib[rows, cols] = acc * shc[rows, :]

    own_tokens = [
        pltpu.make_async_copy(tok.at[pl.ds(half * HALF, HALF), :], tokbuf.at[pl.ds(place[half, 0], HALF), :], own_sem.at[3 + half])
        for half in range(2)
    ]
    small = [pltpu.make_async_copy(ids_hbm, ids, in_sem.at[0]), pltpu.make_async_copy(rw_hbm, rw, in_sem.at[1])]
    for copy in small:
        copy.start()
    for i in range(3):
        own_copy(i).start()
    for copy in own_tokens:
        copy.start()
    for copy in small:
        copy.wait()
    make_shares()
    pl.semaphore_wait(barrier, len(peers))

    ag_first(0)
    for dirn in range(2):
        share_copy(dirn, 1).start()
    ag_first(1)
    for i in range(2):
        for side in range(2):
            x_copy(i, side).start()

    def spread(half, t, q):
        for dirn in range(2):
            if ag_has(dirn, t, q):
                ag_copy(dirn, t, half, q).wait_recv()
            if t < nh and ag_has(dirn, t + 1, q):
                ag_copy(dirn, t + 1, half, q).start()

    def spread_shares(t):
        for dirn in range(2):
            if share_has(dirn, t):
                share_copy(dirn, t).wait_recv()
            if t < nh and share_has(dirn, t + 1):
                share_copy(dirn, t + 1).start()

    copies, products = [], []

    def step(hop):
        for queue in (copies, products):
            if queue and queue[0][0] <= hop:
                call = queue.pop(0)
                call[1](*call[2:])

    def arrive_both(role):
        arrive(0, role)
        arrive(1, role)

    def own_arrived():
        for copy in own_tokens:
            copy.wait()
        arrive_both(0)

    def start_sib(i, k):
        sib_copy(i, k).start()

    def start_down():
        for side in range(2):
            x_copy(2, side).start()

    def arrive_down():
        for role in range(4):
            arrive(2, role)

    for k in range(4):
        for i in range(2):
            copies.append((1, start_sib, i, k))
    copies.append((2, start_down))
    for k in range(4):
        copies.append((3, start_sib, 2, k))
    for i in range(2):
        for side in range(2):
            copies.append((4.2, forward, i, side))
    for side in range(2):
        copies.append((6.3, forward, 2, side))

    products.append((4, own_arrived))
    products.append((4.1, arrive_both, 1))
    for role in range(2):
        for half in range(2):
            products.append((4.1 + half * 0.2, hidden, ("A0", "A1")[half], role))
    for half in range(2):
        products.append((5.2, hidden, ("A0", "A1")[half], 2))
    products.append((6, arrive_both, 3))
    for half in range(2):
        products.append((6, hidden, ("A0", "A1")[half], 3))
    for role in range(4):
        products.append((6.3, hidden, "B", role))
    products.append((6.3, take_shares, order[:nh + nh // 2]))

    for t in range(1, nh):
        for half in range(2):
            for q in range(2):
                spread(half, t, q)
                if half == 0 and q == 1:
                    spread_shares(t)
                step(t + 0.1 * (2 * half + q))
    while copies or products:
        step(nh)

    for role in range(4):
        hidden("C", role)
    arrive_down()
    take_shares(late)
    for n in range(4):
        project("C", n)
    for half in range(2):
        rs_hop(0, 2, half, 0)
        rs_hop(1, 2, half, 1)
    for n in range(4):
        project("B", n)
    for half in range(2):
        for q in range(2):
            spread(half, nh, q)
    spread_shares(nh)
    for role in range(4):
        hidden("D", role)
    take_shares(last)
    for n in range(4):
        project("D", n)
    for half in range(2):
        rs_hop(0, 1, half, 1)
        rs_hop(1, 1, half, 0)

    def sent():
        for half in range(2):
            for tt in range(1, nh + 1):
                for q in range(2):
                    for dirn in range(2):
                        if ag_has(dirn, tt, q):
                            ag_copy(dirn, tt, half, q).wait_send()

    def weights_sent():
        for i in range(3):
            for k in range(4):
                sib_copy(i, k).wait_send()
                fw_copy(i, k).wait_send()
            for side in range(2):
                x_copy(i, side).wait_send()
        for tt in range(1, nh + 1):
            for dirn in range(2):
                if share_has(dirn, tt):
                    share_copy(dirn, tt).wait_send()

    for half in range(2):
        for n in range(4):
            products.append((2, project, ("A0", "A1")[half], n))
    products.append((5, sent))
    products.append((5, weights_sent))

    for t in range(2, nh + 1):
        for half in range(2):
            if t < nh:
                rs_hop(0, t + 1, half, 0)
                rs_hop(1, t + 1, half, 1)
            step(t)
            rs_hop(0, t, half, 1)
            rs_hop(1, t, half, 0)
            step(t)
    for half in range(2):
        for q in range(2):
            rs_last(half, q)
    for half in range(2):
        for t in range(1, nh + 1):
            for q in range(2):
                for dirn in range(2):
                    if rs_has(dirn, t, q):
                        rs_copy(dirn, t, half, q).wait_send()
    for half in range(2):
        for q in range(2):
            out_copy(half, q).wait()


def solution(mesh):
    nz = mesh.shape["expert"] // 4
    nh = nz // 2

    def on_device(tokens, gate, up, down, ids, rw):
        rows, features = tokens.shape
        hdev = gate.shape[1]
        dma = pltpu.SemaphoreType.DMA
        flops = 2 * rows * nz * features * 4 * hdev * 3
        return pl.pallas_call(
            functools.partial(kernel, nz),
            out_shape=jax.ShapeDtypeStruct((rows, features), jnp.bfloat16),
            in_specs=[pl.BlockSpec(memory_space=pl.ANY)] * 6,
            out_specs=pl.BlockSpec(memory_space=pl.ANY),
            scratch_shapes=[
                pltpu.VMEM((nz * rows, features), jnp.bfloat16),
                pltpu.VMEM((2, nz + 1, HALF, features), jnp.bfloat16),
                pltpu.VMEM((nz * rows, features), jnp.float32),
                pltpu.VMEM((nz * rows, 4 * hdev), jnp.bfloat16),
                pltpu.VMEM((4, features, hdev), jnp.bfloat16),
                pltpu.VMEM((4, features, hdev), jnp.bfloat16),
                pltpu.VMEM((4 * hdev, features), jnp.bfloat16),
                pltpu.VMEM((nz, 8, 128), jnp.float32),
                pltpu.VMEM((nz * rows, 1), jnp.float32),
                pltpu.VMEM((ids.shape[1], rows), jnp.int32),
                pltpu.VMEM((ids.shape[1], rows), jnp.float32),
                pltpu.VMEM((rows, features), jnp.bfloat16),
                dma((2, nh, 4)),
                dma((2, nh, 4)),
                dma((2, nh, 4)),
                dma((2, nh, 4)),
                dma((5,)),
                dma((3, 4)),
                dma((3, 4)),
                dma((3, 2)),
                dma((3, 2)),
                dma((3, 4)),
                dma((3, 4)),
                dma((2, nh)),
                dma((2, nh)),
                dma((2,)),
                dma((4,)),
            ],
            compiler_params=pltpu.CompilerParams(
                collective_id=0, has_side_effects=True, vmem_limit_bytes=56 * 1024 * 1024
            ),
            cost_estimate=pl.CostEstimate(flops=flops, bytes_accessed=4 * 1024 * 1024, transcendentals=0),
        )(tokens, gate, up, down, ids.T, rw.T)

    return jax.shard_map(
        on_device,
        mesh=mesh,
        in_specs=(
            P(("dp", "expert"), None),
            P(None, "expert"),
            P(None, "expert"),
            P("expert", None),
            P(("dp", "expert"), None),
            P(("dp", "expert"), None),
        ),
        out_specs=P(("dp", "expert"), None),
        check_vma=False,
    )
```

```python
import functools

import jax
import jax.numpy as jnp
from jax import lax
from jax.experimental import pallas as pl
from jax.experimental.pallas import tpu as pltpu
from jax.sharding import PartitionSpec as P

CAP = 32
Q = 16
HALF = 32
MESH = pl.DeviceIdType.MESH


def kernel(nz, tok, gate, up, down, ids_hbm, rw_hbm, out, tokbuf, rs, contrib, hid, gb, ub, wb, shr, shc, ids, rw,
           pk, pk_back, pk_in, oh, oht,
           ag_send, ag_recv, rs_send, rs_recv, own_sem, sib_send, sib_recv, x_send, x_recv, fw_send, fw_recv,
           sh_send, sh_recv, in_sem):
    nh = nz // 2
    full = (nh - 1, nh - 2)
    packer, packed = (nh - 1, nh + 2), (nh, nh + 1)
    order = [0] + [s for t in range(1, nh - 1) for s in (t, nz - t)] + [nh - 1]
    early, middle, late = order[:nh], order[nh:nh + nh // 2], order[nh + nh // 2:]
    place, tiles, row = {}, {}, 0
    for name, blocks in (
        ("A0", [(0, slot) for slot in early]),
        ("A1", [(1, slot) for slot in early]),
        ("B", [(half, slot) for half in range(2) for slot in middle]),
        ("C", [(half, slot) for slot in late for half in range(2)] + [packed[1]]),
        ("D", [packed[0]]),
    ):
        tiles[name] = (row, len(blocks) * HALF)
        for block in blocks:
            place[block] = row
            row += HALF
    features = tok.shape[1]
    hdev = gate.shape[1]
    d = lax.axis_index("dp")
    e = lax.axis_index("expert")
    z = e // 4
    core = lax.rem(e, 2)
    x_lo = lax.rem(e // 2, 2)
    x_hi = lax.rem(d, 2)
    n_exp = 4 * nz
    way = 1 - 2 * core
    targets = (lax.rem(e + n_exp + 4 * way, n_exp), lax.rem(e + n_exp - 4 * way, n_exp))
    next_plane = (lax.rem(z + nz + way, nz), lax.rem(z + nz - way, nz))
    sib = e + 1 - 2 * core
    xq = e + 2 - 4 * x_lo
    d_other = d + 1 - 2 * x_hi

    def dev(dd, ee):
        return {"dp": dd, "expert": ee}

    barrier = pltpu.get_barrier_semaphore()
    peers = [(d, targets[0]), (d, targets[1]), (d, xq), (d_other, xq), (d, sib)]
    for dd, ee in peers:
        pl.semaphore_signal(barrier, inc=1, device_id=dev(dd, ee), device_id_type=MESH)

    def ag_copy(dirn, t, half, q):
        src_slot, dst_slot = (t - 1, t) if dirn == 0 else ((nz - t + 1) % nz, nz - t)
        if t == 1:
            src = tok.at[pl.ds(half * HALF + q * Q, Q), :]
        else:
            src = tokbuf.at[pl.ds(place[half, src_slot] + q * Q, Q), :]
        i = half * 2 + q
        return pltpu.make_async_remote_copy(
            src_ref=src,
            dst_ref=tokbuf.at[pl.ds(place[half, dst_slot] + q * Q, Q), :],
            send_sem=ag_send.at[dirn, t - 1, i],
            recv_sem=ag_recv.at[dirn, t - 1, i],
            device_id=dev(d, targets[dirn]),
            device_id_type=MESH,
        )

    def pack_copy(dirn):
        return pltpu.make_async_remote_copy(
            src_ref=pk.at[dirn],
            dst_ref=tokbuf.at[pl.ds(place[packed[dirn]], CAP), :],
            send_sem=ag_send.at[dirn, full[dirn], 0],
            recv_sem=ag_recv.at[dirn, full[dirn], 0],
            device_id=dev(d, targets[dirn]),
            device_id_type=MESH,
        )

    def ag_first(half):
        for q in range(2):
            for dirn in range(2):
                ag_copy(dirn, 1, half, q).start()

    def back_copy(dirn):
        return pltpu.make_async_remote_copy(
            src_ref=pk_back.at[dirn],
            dst_ref=pk_in.at[dirn],
            send_sem=rs_send.at[dirn, 0, 0],
            recv_sem=rs_recv.at[dirn, 0, 0],
            device_id=dev(d, targets[1 - dirn]),
            device_id_type=MESH,
        )

    def rs_slots(dirn, t):
        return (nh + 1 - t, nh - t) if dirn == 0 else (nh + t, nh + 1 + t)

    def rs_copy(dirn, t, half, q):
        src_slot, dst_slot = rs_slots(dirn, t)
        i = half * 2 + q
        return pltpu.make_async_remote_copy(
            src_ref=rs.at[half, src_slot, pl.ds(q * Q, Q), :],
            dst_ref=rs.at[half, dst_slot, pl.ds(q * Q, Q), :],
            send_sem=rs_send.at[dirn, t - 1, i],
            recv_sem=rs_recv.at[dirn, t - 1, i],
            device_id=dev(d, targets[1 - dirn]),
            device_id_type=MESH,
        )

    def rs_hop(dirn, t, half, q):
        slot = rs_slots(dirn, t)[0]
        rows = pl.ds(q * Q, Q)
        total = contrib[pl.ds(place[half, slot] + q * Q, Q), :]
        if t > 2:
            rs_copy(dirn, t - 1, half, q).wait_recv()
            total = total + rs[half, slot, rows, :].astype(jnp.float32)
        rs[half, slot, rows, :] = total.astype(jnp.bfloat16)
        rs_copy(dirn, t, half, q).start()

    def rs_last(half, q):
        rows = pl.ds(q * Q, Q)
        rs_copy(0, nh, half, q).wait_recv()
        rs_copy(1, nh - 1, half, q).wait_recv()
        total = contrib[pl.ds(place[half, 0] + q * Q, Q), :]
        total = total + rs[half, 0, rows, :].astype(jnp.float32) + rs[half, nz, rows, :].astype(jnp.float32)
        out[pl.ds(half * HALF + q * Q, Q), :] = total.astype(jnp.bfloat16)

    sources = (gate, up, down)

    def whole(i, role):
        if i == 2:
            return wb.at[pl.ds(role * hdev, hdev), :]
        return (gb, ub)[i].at[role]

    def part(i, role, side):
        if i == 2:
            return wb.at[pl.ds(role * hdev + side * (hdev // 2), hdev // 2), :]
        return (gb, ub)[i].at[role, pl.ds(side * (features // 2), features // 2), :]

    def own_copy(i):
        return pltpu.make_async_copy(sources[i], whole(i, 0), own_sem.at[i])

    def piece(i, role, k):
        size = sources[i].shape[0] // 4
        if i == 2:
            return wb.at[pl.ds(role * hdev + k * size, size), :]
        return (gb, ub)[i].at[role, pl.ds(k * size, size), :]

    def sib_copy(i, k):
        size = sources[i].shape[0] // 4
        return pltpu.make_async_remote_copy(
            src_ref=sources[i].at[pl.ds(k * size, size), :], dst_ref=piece(i, 1, k),
            send_sem=sib_send.at[i, k], recv_sem=sib_recv.at[i, k],
            device_id=dev(d, sib), device_id_type=MESH)

    def x_copy(i, side):
        size = sources[i].shape[0] // 2
        return pltpu.make_async_remote_copy(
            src_ref=sources[i].at[pl.ds(side * size, size), :], dst_ref=part(i, 2, side),
            send_sem=x_send.at[i, side], recv_sem=x_recv.at[i, side],
            device_id=dev(d if side == 0 else d_other, xq), device_id_type=MESH)

    def fw_copy(i, k):
        return pltpu.make_async_remote_copy(
            src_ref=piece(i, 2, k), dst_ref=piece(i, 3, k),
            send_sem=fw_send.at[i, k], recv_sem=fw_recv.at[i, k],
            device_id=dev(d, sib), device_id_type=MESH)

    def forward(i, side):
        x_copy(i, side).wait_recv()
        for k in range(2):
            fw_copy(i, side * 2 + k).start()

    def arrive(i, role):
        if role == 0:
            own_copy(i).wait()
        for k in range(4):
            if role == 1:
                sib_copy(i, k).wait_recv()
            elif role == 3:
                fw_copy(i, k).wait_recv()

    def share_has(dirn, t):
        return t < nh or dirn == 0

    def share_copy(dirn, t):
        src_slot, dst_slot = (t - 1, t) if dirn == 0 else ((nz - t + 1) % nz, nz - t)
        return pltpu.make_async_remote_copy(
            src_ref=shr.at[src_slot], dst_ref=shr.at[dst_slot],
            send_sem=sh_send.at[dirn, t - 1], recv_sem=sh_recv.at[dirn, t - 1],
            device_id=dev(d, targets[dirn]), device_id_type=MESH)

    def make_shares():
        experts = lax.broadcasted_iota(jnp.int32, (nz, 64), 0)
        counts = jnp.zeros((nz, 64), jnp.float32)
        raw = jnp.zeros((nz, 64), jnp.float32)
        for k in range(ids.shape[0]):
            match = ids[k:k + 1, :] == experts
            counts = counts + jnp.where(match, 1.0, 0.0)
            raw = raw + jnp.where(match, rw[k:k + 1, :], 0.0)
        before = lax.broadcasted_iota(jnp.int32, (64, 64), 0) < lax.broadcasted_iota(jnp.int32, (64, 64), 1)
        places = jnp.dot(counts.astype(jnp.bfloat16), jnp.where(before, 1.0, 0.0).astype(jnp.bfloat16),
                         preferred_element_type=jnp.float32)
        shares = jnp.where((counts == 1.0) & (places < CAP), raw, 0.0)
        for k in range(nz // 8):
            shr[0, :, k * 64:(k + 1) * 64] = shares[k * 8:(k + 1) * 8, :]

    def take_shares(slots):
        lane = lax.broadcasted_iota(jnp.int32, (64, 128), 1)
        row = lax.broadcasted_iota(jnp.int32, (64, 128), 0)
        diag = lane == row + 64 * (z // 8)
        for slot in slots:
            mine = shr[slot, pl.ds(lax.rem(z, 8), 1), :]
            column = jnp.sum(jnp.where(diag, mine, 0.0), axis=1, keepdims=True)
            for half in range(2):
                shc[pl.ds(place[half, slot], HALF), :] = column[half * HALF:(half + 1) * HALF]

    def chosen(slot, expert):
        both = shr[slot, pl.ds(lax.rem(expert, 8), 1), :]
        share = jnp.where(expert >= 8, both[:, 64:], both[:, :64])
        kept = jnp.where(share > 0.0, 1.0, 0.0)
        before = lax.broadcasted_iota(jnp.int32, (64, 64), 0) < lax.broadcasted_iota(jnp.int32, (64, 64), 1)
        place_of = jnp.dot(jnp.broadcast_to(kept, (16, 64)).astype(jnp.bfloat16), jnp.where(before, 1.0, 0.0).astype(jnp.bfloat16),
                           preferred_element_type=jnp.float32)[:1]
        place_of = jnp.where(kept > 0.0, place_of, -1.0)
        slots = lax.broadcasted_iota(jnp.int32, (CAP, 64), 0).astype(jnp.float32)
        return share, place_of, jnp.where(slots == place_of, 1.0, 0.0)

    def prepare(dirn):
        share, place_of, pick = chosen(packer[dirn], next_plane[dirn])
        oh[dirn, :, :] = pick.astype(jnp.bfloat16)
        diag = lax.broadcasted_iota(jnp.int32, (64, 64), 0) == lax.broadcasted_iota(jnp.int32, (64, 64), 1)
        column = jnp.sum(jnp.where(diag, place_of, 0.0), axis=1, keepdims=True)
        slots = lax.broadcasted_iota(jnp.int32, (64, CAP), 1).astype(jnp.float32)
        oht[dirn, :, :] = jnp.where(slots == column, 1.0, 0.0).astype(jnp.bfloat16)

    def pack(dirn):
        block = tokbuf[pl.ds(place[0, packer[dirn]], 2 * HALF), :]
        pk[dirn, :, :] = jnp.dot(oh[dirn], block, preferred_element_type=jnp.float32).astype(jnp.bfloat16)
        pack_copy(dirn).start()

    def take_packed_shares(dirn):
        share, place_of, pick = chosen(packed[dirn], z)
        shc[pl.ds(place[packed[dirn]], CAP), :] = jnp.sum(pick * share, axis=1, keepdims=True)

    def send_back(dirn):
        pk_back[dirn, :, :] = contrib[pl.ds(place[packed[dirn]], CAP), :].astype(jnp.bfloat16)
        back_copy(dirn).start()

    def unpack(dirn):
        back_copy(dirn).wait_recv()
        rows = pl.ds(place[0, packer[dirn]], 2 * HALF)
        contrib[rows, :] = contrib[rows, :] + jnp.dot(oht[dirn], pk_in[dirn], preferred_element_type=jnp.float32)
        for half in range(2):
            for q in range(2):
                rs_hop(dirn, 2, half, q)

    def hidden(m, role):
        rows = pl.ds(*tiles[m])
        x = tokbuf[rows, :]
        g = jnp.dot(x, gb[role], preferred_element_type=jnp.float32)
        v = jnp.dot(x, ub[role], preferred_element_type=jnp.float32)
        hid[rows, role * hdev:(role + 1) * hdev] = (g / (1.0 + jnp.exp(-g)) * v).astype(jnp.bfloat16)

    def project(m, n):
        rows = pl.ds(*tiles[m])
        width = features // 4
        cols = slice(n * width, (n + 1) * width)
        acc = jnp.dot(hid[rows, :], wb[:, cols], preferred_element_type=jnp.float32)
        contrib[rows, cols] = acc * shc[rows, :]

    own_tokens = [
        pltpu.make_async_copy(tok.at[pl.ds(half * HALF, HALF), :], tokbuf.at[pl.ds(place[half, 0], HALF), :], own_sem.at[3 + half])
        for half in range(2)
    ]
    small = [pltpu.make_async_copy(ids_hbm, ids, in_sem.at[0]), pltpu.make_async_copy(rw_hbm, rw, in_sem.at[1])]
    for copy in small:
        copy.start()
    for i in range(3):
        own_copy(i).start()
    for copy in own_tokens:
        copy.start()
    for copy in small:
        copy.wait()
    make_shares()
    pl.semaphore_wait(barrier, len(peers))

    ag_first(0)
    for dirn in range(2):
        share_copy(dirn, 1).start()
    ag_first(1)
    for i in range(2):
        for side in range(2):
            x_copy(i, side).start()

    def spread(half, t, q):
        for dirn in range(2):
            if t <= full[dirn]:
                ag_copy(dirn, t, half, q).wait_recv()
            if t + 1 <= full[dirn]:
                ag_copy(dirn, t + 1, half, q).start()

    def spread_shares(t):
        for dirn in range(2):
            if share_has(dirn, t):
                share_copy(dirn, t).wait_recv()
            if t < nh and share_has(dirn, t + 1):
                share_copy(dirn, t + 1).start()

    copies, products = [], []

    def step(hop):
        for queue in (copies, products):
            if queue and queue[0][0] <= hop:
                call = queue.pop(0)
                call[1](*call[2:])

    def arrive_both(role):
        arrive(0, role)
        arrive(1, role)

    def own_arrived():
        for copy in own_tokens:
            copy.wait()
        arrive_both(0)

    def start_sib(i, k):
        sib_copy(i, k).start()

    def start_down():
        for side in range(2):
            x_copy(2, side).start()

    def arrive_down():
        for role in range(4):
            arrive(2, role)

    for k in range(4):
        for i in range(2):
            copies.append((1, start_sib, i, k))
    copies.append((2, start_down))
    for k in range(4):
        copies.append((3, start_sib, 2, k))
    for i in range(2):
        for side in range(2):
            copies.append((4.2, forward, i, side))
    for side in range(2):
        copies.append((6.3, forward, 2, side))

    products.append((4, own_arrived))
    products.append((4.1, arrive_both, 1))
    for role in range(2):
        for half in range(2):
            products.append((4.1 + half * 0.2, hidden, ("A0", "A1")[half], role))
    for half in range(2):
        products.append((5.2, hidden, ("A0", "A1")[half], 2))
    products.append((6, arrive_both, 3))
    for half in range(2):
        products.append((6, hidden, ("A0", "A1")[half], 3))
    for role in range(4):
        products.append((6.3, hidden, "B", role))
    products.append((6.3, take_shares, order[:nh + nh // 2]))

    for t in range(1, nh):
        for half in range(2):
            for q in range(2):
                spread(half, t, q)
                if half == 0 and q == 1:
                    spread_shares(t)
                    for dirn in range(2):
                        if t == full[dirn]:
                            prepare(dirn)
                for dirn in range(2):
                    if (t, half, q) == (full[dirn], 1, 1):
                        pack(dirn)
                step(t + 0.1 * (2 * half + q))
    while copies or products:
        step(nh)

    pack_copy(1).wait_recv()
    for role in range(4):
        hidden("C", role)
    arrive_down()
    take_shares(late)
    take_packed_shares(1)
    for n in range(4):
        project("C", n)
    send_back(1)
    spread_shares(nh)
    pack_copy(0).wait_recv()
    for role in range(4):
        hidden("D", role)
    take_packed_shares(0)
    for n in range(4):
        project("D", n)
    send_back(0)
    unpack(1)
    for n in range(4):
        project("B", n)
    unpack(0)

    def sent():
        for half in range(2):
            for tt in range(1, nh + 1):
                for q in range(2):
                    for dirn in range(2):
                        if tt <= full[dirn]:
                            ag_copy(dirn, tt, half, q).wait_send()

        for dirn in range(2):
            pack_copy(dirn).wait_send()
            back_copy(dirn).wait_send()

    def weights_sent():
        for i in range(3):
            for k in range(4):
                sib_copy(i, k).wait_send()
                fw_copy(i, k).wait_send()
            for side in range(2):
                x_copy(i, side).wait_send()
        for tt in range(1, nh + 1):
            for dirn in range(2):
                if share_has(dirn, tt):
                    share_copy(dirn, tt).wait_send()

    for half in range(2):
        for n in range(4):
            products.append((2, project, ("A0", "A1")[half], n))
    products.append((5, sent))
    products.append((5, weights_sent))

    for t in range(3, nh + 1):
        for half in range(2):
            for q in range(2):
                if t < nh:
                    rs_hop(1, t, half, q)
                step(t)
                rs_hop(0, t, half, q)
    for half in range(2):
        for q in range(2):
            rs_last(half, q)
    for half in range(2):
        for t in range(1, nh + 1):
            for q in range(2):
                for dirn in range(2):
                    if 1 < t <= nh - dirn:
                        rs_copy(dirn, t, half, q).wait_send()


def solution(mesh):
    nz = mesh.shape["expert"] // 4
    nh = nz // 2

    def on_device(tokens, gate, up, down, ids, rw):
        rows, features = tokens.shape
        hdev = gate.shape[1]
        dma = pltpu.SemaphoreType.DMA
        flops = 2 * rows * nz * features * 4 * hdev * 3
        return pl.pallas_call(
            functools.partial(kernel, nz),
            out_shape=pltpu.VMEM((rows, features), jnp.bfloat16),
            in_specs=[pl.BlockSpec(memory_space=pl.ANY)] * 6,
            out_specs=pl.BlockSpec(memory_space=pltpu.VMEM),
            scratch_shapes=[
                pltpu.VMEM((nz * rows, features), jnp.bfloat16),
                pltpu.VMEM((2, nz + 1, HALF, features), jnp.bfloat16),
                pltpu.VMEM((nz * rows, features), jnp.float32),
                pltpu.VMEM((nz * rows, 4 * hdev), jnp.bfloat16),
                pltpu.VMEM((4, features, hdev), jnp.bfloat16),
                pltpu.VMEM((4, features, hdev), jnp.bfloat16),
                pltpu.VMEM((4 * hdev, features), jnp.bfloat16),
                pltpu.VMEM((nz, 8, 128), jnp.float32),
                pltpu.VMEM((nz * rows, 1), jnp.float32),
                pltpu.VMEM((ids.shape[1], rows), jnp.int32),
                pltpu.VMEM((ids.shape[1], rows), jnp.float32),
                pltpu.VMEM((2, CAP, features), jnp.bfloat16),
                pltpu.VMEM((2, CAP, features), jnp.bfloat16),
                pltpu.VMEM((2, CAP, features), jnp.bfloat16),
                pltpu.VMEM((2, CAP, rows), jnp.bfloat16),
                pltpu.VMEM((2, rows, CAP), jnp.bfloat16),
                dma((2, nh, 4)),
                dma((2, nh, 4)),
                dma((2, nh, 4)),
                dma((2, nh, 4)),
                dma((5,)),
                dma((3, 4)),
                dma((3, 4)),
                dma((3, 2)),
                dma((3, 2)),
                dma((3, 4)),
                dma((3, 4)),
                dma((2, nh)),
                dma((2, nh)),
                dma((2,)),
            ],
            compiler_params=pltpu.CompilerParams(
                collective_id=0, has_side_effects=True, vmem_limit_bytes=56 * 1024 * 1024
            ),
            cost_estimate=pl.CostEstimate(flops=flops, bytes_accessed=4 * 1024 * 1024, transcendentals=0),
        )(tokens, gate, up, down, ids.T, rw.T)

    return jax.shard_map(
        on_device,
        mesh=mesh,
        in_specs=(
            P(("dp", "expert"), None),
            P(None, "expert"),
            P(None, "expert"),
            P("expert", None),
            P(("dp", "expert"), None),
            P(("dp", "expert"), None),
        ),
        out_specs=P(("dp", "expert"), None),
        check_vma=False,
    )
```

```python
import functools

import jax
import jax.numpy as jnp
from jax import lax
from jax.experimental import pallas as pl
from jax.experimental.pallas import tpu as pltpu
from jax.sharding import PartitionSpec as P

CAP = 32
Q = 16
HALF = 32
PIECES = 4
MESH = pl.DeviceIdType.MESH


def kernel(nz, tok, gate, up, down, ids_hbm, rw_hbm, out, tokbuf, rs, contrib, hid, gb, ub, wb, shr, shc, ids, rw,
           pk, pk_back, pk_in, oh, oht,
           ag_send, ag_recv, rs_send, rs_recv, own_sem, sib_send, sib_recv, x_send, x_recv, fw_send, fw_recv,
           sh_send, sh_recv, in_sem):
    nh = nz // 2
    full = (nh - 1, nh - 2)
    packer, packed = (nh - 1, nh + 2), (nh, nh + 1)
    order = [0] + [s for t in range(1, nh - 1) for s in (t, nz - t)] + [nh - 1]
    early, middle, late = order[:nh], order[nh:nh + nh // 2], order[nh + nh // 2:]
    place, tiles, row = {}, {}, 0
    for name, blocks in (
        ("A0", [(0, slot) for slot in early]),
        ("A1", [(1, slot) for slot in early]),
        ("B", [(half, slot) for half in range(2) for slot in middle]),
        ("C", [(half, packer[1]) for half in range(2)] + [packed[1]]),
        ("D", [(half, packer[0]) for half in range(2)] + [packed[0]]),
    ):
        tiles[name] = (row, len(blocks) * HALF)
        for block in blocks:
            place[block] = row
            row += HALF
    features = tok.shape[1]
    hdev = gate.shape[1]
    d = lax.axis_index("dp")
    e = lax.axis_index("expert")
    z = e // 4
    core = lax.rem(e, 2)
    x_lo = lax.rem(e // 2, 2)
    x_hi = lax.rem(d, 2)
    n_exp = 4 * nz
    way = 1 - 2 * core
    targets = (lax.rem(e + n_exp + 4 * way, n_exp), lax.rem(e + n_exp - 4 * way, n_exp))
    next_plane = (lax.rem(z + nz + way, nz), lax.rem(z + nz - way, nz))
    sib = e + 1 - 2 * core
    xq = e + 2 - 4 * x_lo
    d_other = d + 1 - 2 * x_hi

    def dev(dd, ee):
        return {"dp": dd, "expert": ee}

    barrier = pltpu.get_barrier_semaphore()
    peers = [(d, targets[0]), (d, targets[1]), (d, xq), (d_other, xq), (d, sib)]
    for dd, ee in peers:
        pl.semaphore_signal(barrier, inc=1, device_id=dev(dd, ee), device_id_type=MESH)

    def ag_copy(dirn, t, half, q):
        src_slot, dst_slot = (t - 1, t) if dirn == 0 else ((nz - t + 1) % nz, nz - t)
        if t == 1:
            src = tok.at[pl.ds(half * HALF + q * Q, Q), :]
        else:
            src = tokbuf.at[pl.ds(place[half, src_slot] + q * Q, Q), :]
        i = half * 2 + q
        return pltpu.make_async_remote_copy(
            src_ref=src,
            dst_ref=tokbuf.at[pl.ds(place[half, dst_slot] + q * Q, Q), :],
            send_sem=ag_send.at[dirn, t - 1, i],
            recv_sem=ag_recv.at[dirn, t - 1, i],
            device_id=dev(d, targets[dirn]),
            device_id_type=MESH,
        )

    width = features // PIECES

    def pack_copy(dirn, n):
        cols = pl.ds(n * width, width)
        return pltpu.make_async_remote_copy(
            src_ref=pk.at[dirn, :, cols],
            dst_ref=tokbuf.at[pl.ds(place[packed[dirn]], CAP), cols],
            send_sem=ag_send.at[dirn, full[dirn], n],
            recv_sem=ag_recv.at[dirn, full[dirn], n],
            device_id=dev(d, targets[dirn]),
            device_id_type=MESH,
        )

    def ag_first(half):
        for q in range(2):
            for dirn in range(2):
                ag_copy(dirn, 1, half, q).start()

    def back_copy(dirn, n):
        cols = pl.ds(n * width, width)
        return pltpu.make_async_remote_copy(
            src_ref=pk_back.at[dirn, :, cols],
            dst_ref=pk_in.at[dirn, :, cols],
            send_sem=rs_send.at[dirn, 0, n],
            recv_sem=rs_recv.at[dirn, 0, n],
            device_id=dev(d, targets[1 - dirn]),
            device_id_type=MESH,
        )

    def rs_slots(dirn, t):
        return (nh + 1 - t, nh - t) if dirn == 0 else (nh + t, nh + 1 + t)

    def rs_copy(dirn, t, half, q):
        src_slot, dst_slot = rs_slots(dirn, t)
        i = half * 2 + q
        return pltpu.make_async_remote_copy(
            src_ref=rs.at[half, src_slot, pl.ds(q * Q, Q), :],
            dst_ref=rs.at[half, dst_slot, pl.ds(q * Q, Q), :],
            send_sem=rs_send.at[dirn, t - 1, i],
            recv_sem=rs_recv.at[dirn, t - 1, i],
            device_id=dev(d, targets[1 - dirn]),
            device_id_type=MESH,
        )

    def rs_hop(dirn, t, half, q):
        slot = rs_slots(dirn, t)[0]
        rows = pl.ds(q * Q, Q)
        total = contrib[pl.ds(place[half, slot] + q * Q, Q), :]
        if t > 2:
            rs_copy(dirn, t - 1, half, q).wait_recv()
            total = total + rs[half, slot, rows, :].astype(jnp.float32)
        rs[half, slot, rows, :] = total.astype(jnp.bfloat16)
        rs_copy(dirn, t, half, q).start()
        if t > 3:
            rs_copy(dirn, t - 2, half, q).wait_send()

    def rs_last(half, q):
        rows = pl.ds(q * Q, Q)
        rs_copy(0, nh, half, q).wait_recv()
        rs_copy(1, nh - 1, half, q).wait_recv()
        total = contrib[pl.ds(place[half, 0] + q * Q, Q), :]
        total = total + rs[half, 0, rows, :].astype(jnp.float32) + rs[half, nz, rows, :].astype(jnp.float32)
        out[pl.ds(half * HALF + q * Q, Q), :] = total.astype(jnp.bfloat16)

    sources = (gate, up, down)

    def whole(i, role):
        if i == 2:
            return wb.at[pl.ds(role * hdev, hdev), :]
        return (gb, ub)[i].at[role]

    def part(i, role, side):
        if i == 2:
            return wb.at[pl.ds(role * hdev + side * (hdev // 2), hdev // 2), :]
        return (gb, ub)[i].at[role, pl.ds(side * (features // 2), features // 2), :]

    def own_copy(i):
        return pltpu.make_async_copy(sources[i], whole(i, 0), own_sem.at[i])

    def piece(i, role, k):
        size = sources[i].shape[0] // 4
        if i == 2:
            return wb.at[pl.ds(role * hdev + k * size, size), :]
        return (gb, ub)[i].at[role, pl.ds(k * size, size), :]

    def sib_copy(i, k):
        size = sources[i].shape[0] // 4
        return pltpu.make_async_remote_copy(
            src_ref=sources[i].at[pl.ds(k * size, size), :], dst_ref=piece(i, 1, k),
            send_sem=sib_send.at[i, k], recv_sem=sib_recv.at[i, k],
            device_id=dev(d, sib), device_id_type=MESH)

    def x_copy(i, side):
        size = sources[i].shape[0] // 2
        return pltpu.make_async_remote_copy(
            src_ref=sources[i].at[pl.ds(side * size, size), :], dst_ref=part(i, 2, side),
            send_sem=x_send.at[i, side], recv_sem=x_recv.at[i, side],
            device_id=dev(d if side == 0 else d_other, xq), device_id_type=MESH)

    def fw_copy(i, k):
        return pltpu.make_async_remote_copy(
            src_ref=piece(i, 2, k), dst_ref=piece(i, 3, k),
            send_sem=fw_send.at[i, k], recv_sem=fw_recv.at[i, k],
            device_id=dev(d, sib), device_id_type=MESH)

    def forward(i, side):
        x_copy(i, side).wait_recv()
        for k in range(2):
            fw_copy(i, side * 2 + k).start()

    def arrive(i, role):
        if role == 0:
            own_copy(i).wait()
        for k in range(4):
            if role == 1:
                sib_copy(i, k).wait_recv()
            elif role == 3:
                fw_copy(i, k).wait_recv()

    def share_has(dirn, t):
        return t < nh or dirn == 0

    def share_copy(dirn, t):
        src_slot, dst_slot = (t - 1, t) if dirn == 0 else ((nz - t + 1) % nz, nz - t)
        return pltpu.make_async_remote_copy(
            src_ref=shr.at[src_slot], dst_ref=shr.at[dst_slot],
            send_sem=sh_send.at[dirn, t - 1], recv_sem=sh_recv.at[dirn, t - 1],
            device_id=dev(d, targets[dirn]), device_id_type=MESH)

    def make_shares():
        experts = lax.broadcasted_iota(jnp.int32, (nz, 64), 0)
        counts = jnp.zeros((nz, 64), jnp.float32)
        raw = jnp.zeros((nz, 64), jnp.float32)
        for k in range(ids.shape[0]):
            match = ids[k:k + 1, :] == experts
            counts = counts + jnp.where(match, 1.0, 0.0)
            raw = raw + jnp.where(match, rw[k:k + 1, :], 0.0)
        before = lax.broadcasted_iota(jnp.int32, (64, 64), 0) < lax.broadcasted_iota(jnp.int32, (64, 64), 1)
        places = jnp.dot(counts.astype(jnp.bfloat16), jnp.where(before, 1.0, 0.0).astype(jnp.bfloat16),
                         preferred_element_type=jnp.float32)
        shares = jnp.where((counts == 1.0) & (places < CAP), raw, 0.0)
        for k in range(nz // 8):
            shr[0, :, k * 64:(k + 1) * 64] = shares[k * 8:(k + 1) * 8, :]

    def take_shares(slots):
        lane = lax.broadcasted_iota(jnp.int32, (64, 128), 1)
        row = lax.broadcasted_iota(jnp.int32, (64, 128), 0)
        diag = lane == row + 64 * (z // 8)
        for slot in slots:
            mine = shr[slot, pl.ds(lax.rem(z, 8), 1), :]
            column = jnp.sum(jnp.where(diag, mine, 0.0), axis=1, keepdims=True)
            for half in range(2):
                shc[pl.ds(place[half, slot], HALF), :] = column[half * HALF:(half + 1) * HALF]

    def chosen(slot, expert):
        both = shr[slot, pl.ds(lax.rem(expert, 8), 1), :]
        share = jnp.where(expert >= 8, both[:, 64:], both[:, :64])
        kept = jnp.where(share > 0.0, 1.0, 0.0)
        before = lax.broadcasted_iota(jnp.int32, (64, 64), 0) < lax.broadcasted_iota(jnp.int32, (64, 64), 1)
        place_of = jnp.dot(jnp.broadcast_to(kept, (16, 64)).astype(jnp.bfloat16), jnp.where(before, 1.0, 0.0).astype(jnp.bfloat16),
                           preferred_element_type=jnp.float32)[:1]
        place_of = jnp.where(kept > 0.0, place_of, -1.0)
        slots = lax.broadcasted_iota(jnp.int32, (CAP, 64), 0).astype(jnp.float32)
        return share, place_of, jnp.where(slots == place_of, 1.0, 0.0)

    def prepare(dirn):
        share, place_of, pick = chosen(packer[dirn], next_plane[dirn])
        oh[dirn, :, :] = pick.astype(jnp.bfloat16)
        diag = lax.broadcasted_iota(jnp.int32, (64, 64), 0) == lax.broadcasted_iota(jnp.int32, (64, 64), 1)
        column = jnp.sum(jnp.where(diag, place_of, 0.0), axis=1, keepdims=True)
        slots = lax.broadcasted_iota(jnp.int32, (64, CAP), 1).astype(jnp.float32)
        oht[dirn, :, :] = jnp.where(slots == column, 1.0, 0.0).astype(jnp.bfloat16)

    def pack(dirn):
        for n in range(PIECES):
            cols = pl.ds(n * width, width)
            block = tokbuf[pl.ds(place[0, packer[dirn]], 2 * HALF), cols]
            pk[dirn, :, cols] = jnp.dot(oh[dirn], block, preferred_element_type=jnp.float32).astype(jnp.bfloat16)
            pack_copy(dirn, n).start()

    def packed_arrived(dirn):
        for n in range(PIECES):
            pack_copy(dirn, n).wait_recv()

    def take_packed_shares(dirn):
        share, place_of, pick = chosen(packed[dirn], z)
        shc[pl.ds(place[packed[dirn]], CAP), :] = jnp.sum(pick * share, axis=1, keepdims=True)

    def send_back(dirn, n):
        cols = pl.ds(n * width, width)
        pk_back[dirn, :, cols] = contrib[pl.ds(place[packed[dirn]], CAP), cols].astype(jnp.bfloat16)
        back_copy(dirn, n).start()

    def unpack(dirn):
        rows = pl.ds(place[0, packer[dirn]], 2 * HALF)
        for n in range(PIECES):
            back_copy(dirn, n).wait_recv()
            cols = pl.ds(n * width, width)
            contrib[rows, cols] = contrib[rows, cols] + jnp.dot(oht[dirn], pk_in[dirn, :, cols], preferred_element_type=jnp.float32)
        for half in range(2):
            for q in range(2):
                rs_hop(dirn, 2, half, q)

    def hidden(m, role):
        rows = pl.ds(*tiles[m])
        x = tokbuf[rows, :]
        g = jnp.dot(x, gb[role], preferred_element_type=jnp.float32)
        v = jnp.dot(x, ub[role], preferred_element_type=jnp.float32)
        hid[rows, role * hdev:(role + 1) * hdev] = (g / (1.0 + jnp.exp(-g)) * v).astype(jnp.bfloat16)

    def project(m, n):
        rows = pl.ds(*tiles[m])
        cols = slice(n * width, (n + 1) * width)
        acc = jnp.dot(hid[rows, :], wb[:, cols], preferred_element_type=jnp.float32)
        contrib[rows, cols] = acc * shc[rows, :]

    own_tokens = [
        pltpu.make_async_copy(tok.at[pl.ds(half * HALF, HALF), :], tokbuf.at[pl.ds(place[half, 0], HALF), :], own_sem.at[3 + half])
        for half in range(2)
    ]
    small = [pltpu.make_async_copy(ids_hbm, ids, in_sem.at[0]), pltpu.make_async_copy(rw_hbm, rw, in_sem.at[1])]
    for copy in small:
        copy.start()
    for i in range(3):
        own_copy(i).start()
    for copy in own_tokens:
        copy.start()
    for copy in small:
        copy.wait()
    make_shares()
    pl.semaphore_wait(barrier, len(peers))

    ag_first(0)
    for dirn in range(2):
        share_copy(dirn, 1).start()
    ag_first(1)
    for i in range(2):
        for side in range(2):
            x_copy(i, side).start()

    def spread(half, t, q):
        for dirn in range(2):
            if t <= full[dirn]:
                ag_copy(dirn, t, half, q).wait_recv()
            if t + 1 <= full[dirn]:
                ag_copy(dirn, t + 1, half, q).start()

    def spread_shares(t):
        for dirn in range(2):
            if share_has(dirn, t):
                share_copy(dirn, t).wait_recv()
            if t < nh and share_has(dirn, t + 1):
                share_copy(dirn, t + 1).start()

    copies, products = [], []

    def step(hop):
        for queue in (copies, products):
            if queue and queue[0][0] <= hop:
                call = queue.pop(0)
                call[1](*call[2:])

    def arrive_both(role):
        arrive(0, role)
        arrive(1, role)

    def own_arrived():
        for copy in own_tokens:
            copy.wait()
        arrive_both(0)

    def start_sib(i, k):
        sib_copy(i, k).start()

    def start_down():
        for side in range(2):
            x_copy(2, side).start()

    def arrive_down():
        for role in range(4):
            arrive(2, role)

    for k in range(4):
        for i in range(2):
            copies.append((1, start_sib, i, k))
    copies.append((2, start_down))
    for k in range(4):
        copies.append((3, start_sib, 2, k))
    for i in range(2):
        for side in range(2):
            copies.append((4.2, forward, i, side))
    for side in range(2):
        copies.append((6.3, forward, 2, side))

    products.append((4, own_arrived))
    products.append((4.1, arrive_both, 1))
    for role in range(2):
        for half in range(2):
            products.append((4.1 + half * 0.2, hidden, ("A0", "A1")[half], role))
    for half in range(2):
        products.append((5.2, hidden, ("A0", "A1")[half], 2))
    products.append((6, arrive_both, 3))
    for half in range(2):
        products.append((6, hidden, ("A0", "A1")[half], 3))
    for role in range(4):
        products.append((6.3, hidden, "B", role))
    products.append((6.3, take_shares, order[:nh + nh // 2]))

    for t in range(1, nh):
        for half in range(2):
            for q in range(2):
                spread(half, t, q)
                if half == 0 and q == 1:
                    spread_shares(t)
                    for dirn in range(2):
                        if t == full[dirn]:
                            prepare(dirn)
                for dirn in range(2):
                    if (t, half, q) == (full[dirn], 1, 1):
                        pack(dirn)
                step(t + 0.1 * (2 * half + q))
    while copies or products:
        step(nh)

    take_shares(late)
    take_packed_shares(1)
    arrive_down()
    packed_arrived(1)
    for role in range(4):
        hidden("C", role)
    for n in range(PIECES):
        project("C", n)
        send_back(1, n)
    spread_shares(nh)
    take_packed_shares(0)
    packed_arrived(0)
    for role in range(4):
        hidden("D", role)
    for n in range(PIECES):
        project("D", n)
        send_back(0, n)
    unpack(1)
    for n in range(PIECES):
        project("B", n)
    unpack(0)

    done = []
    for tt in range(1, nh + 1):
        for half in range(2):
            for q in range(2):
                for dirn in range(2):
                    if tt <= full[dirn]:
                        done.append(ag_copy(dirn, tt, half, q))
        for dirn in range(2):
            if share_has(dirn, tt):
                done.append(share_copy(dirn, tt))
    for dirn in range(2):
        for n in range(PIECES):
            done.append(pack_copy(dirn, n))
            done.append(back_copy(dirn, n))
    for i in range(3):
        for k in range(4):
            done.append(sib_copy(i, k))
            done.append(fw_copy(i, k))
        for side in range(2):
            done.append(x_copy(i, side))

    def sent(copies):
        for copy in copies:
            copy.wait_send()

    for half in range(2):
        for n in range(4):
            products.append((2, project, ("A0", "A1")[half], n))
    for i in range(0, len(done), 8):
        products.append((4, sent, done[i:i + 8]))

    for t in range(3, nh + 1):
        for half in range(2):
            for q in range(2):
                if t < nh:
                    rs_hop(1, t, half, q)
                step(t)
                rs_hop(0, t, half, q)
    for half in range(2):
        for q in range(2):
            rs_last(half, q)
    while products:
        step(nh + 1)
    for half in range(2):
        for q in range(2):
            for dirn in range(2):
                for t in range(full[dirn], full[dirn] + 2):
                    rs_copy(dirn, t, half, q).wait_send()


def solution(mesh):
    nz = mesh.shape["expert"] // 4
    nh = nz // 2

    def on_device(tokens, gate, up, down, ids, rw):
        rows, features = tokens.shape
        hdev = gate.shape[1]
        dma = pltpu.SemaphoreType.DMA
        flops = 2 * rows * nz * features * 4 * hdev * 3
        return pl.pallas_call(
            functools.partial(kernel, nz),
            out_shape=pltpu.VMEM((rows, features), jnp.bfloat16),
            in_specs=[pl.BlockSpec(memory_space=pl.ANY)] * 6,
            out_specs=pl.BlockSpec(memory_space=pltpu.VMEM),
            scratch_shapes=[
                pltpu.VMEM((nz * rows, features), jnp.bfloat16),
                pltpu.VMEM((2, nz + 1, HALF, features), jnp.bfloat16),
                pltpu.VMEM((nz * rows, features), jnp.float32),
                pltpu.VMEM((nz * rows, 4 * hdev), jnp.bfloat16),
                pltpu.VMEM((4, features, hdev), jnp.bfloat16),
                pltpu.VMEM((4, features, hdev), jnp.bfloat16),
                pltpu.VMEM((4 * hdev, features), jnp.bfloat16),
                pltpu.VMEM((nz, 8, 128), jnp.float32),
                pltpu.VMEM((nz * rows, 1), jnp.float32),
                pltpu.VMEM((ids.shape[1], rows), jnp.int32),
                pltpu.VMEM((ids.shape[1], rows), jnp.float32),
                pltpu.VMEM((2, CAP, features), jnp.bfloat16),
                pltpu.VMEM((2, CAP, features), jnp.bfloat16),
                pltpu.VMEM((2, CAP, features), jnp.bfloat16),
                pltpu.VMEM((2, CAP, rows), jnp.bfloat16),
                pltpu.VMEM((2, rows, CAP), jnp.bfloat16),
                dma((2, nh, 4)),
                dma((2, nh, 4)),
                dma((2, nh, 4)),
                dma((2, nh, 4)),
                dma((5,)),
                dma((3, 4)),
                dma((3, 4)),
                dma((3, 2)),
                dma((3, 2)),
                dma((3, 4)),
                dma((3, 4)),
                dma((2, nh)),
                dma((2, nh)),
                dma((2,)),
            ],
            compiler_params=pltpu.CompilerParams(
                collective_id=0, has_side_effects=True, vmem_limit_bytes=56 * 1024 * 1024
            ),
            cost_estimate=pl.CostEstimate(flops=flops, bytes_accessed=4 * 1024 * 1024, transcendentals=0),
        )(tokens, gate, up, down, ids.T, rw.T)

    return jax.shard_map(
        on_device,
        mesh=mesh,
        in_specs=(
            P(("dp", "expert"), None),
            P(None, "expert"),
            P(None, "expert"),
            P("expert", None),
            P(("dp", "expert"), None),
            P(("dp", "expert"), None),
        ),
        out_specs=P(("dp", "expert"), None),
        check_vma=False,
    )
```

```python
import functools

import jax
import jax.numpy as jnp
from jax import lax
from jax.experimental import pallas as pl
from jax.experimental.pallas import tpu as pltpu
from jax.sharding import PartitionSpec as P

CAP = 32
Q = 16
HALF = 32
PIECES = 2
MESH = pl.DeviceIdType.MESH


def kernel(nz, tok, gate, up, down, ids_hbm, rw_hbm, out, tokbuf, rs, contrib, hid, gb, ub, wb, shr, shc, ids, rw,
           pk, pk_back, pk_in, oh, oht,
           ag_send, ag_recv, rs_send, rs_recv, own_sem, sib_send, sib_recv, x_send, x_recv, fw_send, fw_recv,
           sh_send, sh_recv, in_sem):
    nh = nz // 2
    full = (nh - 1, nh - 2)
    packer, packed = (nh - 1, nh + 2), (nh, nh + 1)
    order = [0] + [s for t in range(1, nh - 1) for s in (t, nz - t)] + [nh - 1]
    early, middle, late = order[:nh], order[nh:nh + nh // 2], order[nh + nh // 2:]
    place, tiles, row = {}, {}, 0
    for name, blocks in (
        ("A0", [(0, slot) for slot in early]),
        ("A1", [(1, slot) for slot in early]),
        ("B", [(half, slot) for half in range(2) for slot in middle]),
        ("C", [(half, packer[1]) for half in range(2)] + [packed[1]]),
        ("D", [(half, packer[0]) for half in range(2)] + [packed[0]]),
    ):
        tiles[name] = (row, len(blocks) * HALF)
        for block in blocks:
            place[block] = row
            row += HALF
    features = tok.shape[1]
    hdev = gate.shape[1]
    d = lax.axis_index("dp")
    e = lax.axis_index("expert")
    z = e // 4
    core = lax.rem(e, 2)
    x_lo = lax.rem(e // 2, 2)
    x_hi = lax.rem(d, 2)
    n_exp = 4 * nz
    way = 1 - 2 * core
    targets = (lax.rem(e + n_exp + 4 * way, n_exp), lax.rem(e + n_exp - 4 * way, n_exp))
    next_plane = (lax.rem(z + nz + way, nz), lax.rem(z + nz - way, nz))
    sib = e + 1 - 2 * core
    xq = e + 2 - 4 * x_lo
    d_other = d + 1 - 2 * x_hi

    def dev(dd, ee):
        return {"dp": dd, "expert": ee}

    barrier = pltpu.get_barrier_semaphore()
    peers = [(d, targets[0]), (d, targets[1]), (d, xq), (d_other, xq), (d, sib)]
    for dd, ee in peers:
        pl.semaphore_signal(barrier, inc=1, device_id=dev(dd, ee), device_id_type=MESH)

    def ag_copy(dirn, t, half, q):
        src_slot, dst_slot = (t - 1, t) if dirn == 0 else ((nz - t + 1) % nz, nz - t)
        if t == 1:
            src = tok.at[pl.ds(half * HALF + q * Q, Q), :]
        else:
            src = tokbuf.at[pl.ds(place[half, src_slot] + q * Q, Q), :]
        i = half * 2 + q
        return pltpu.make_async_remote_copy(
            src_ref=src,
            dst_ref=tokbuf.at[pl.ds(place[half, dst_slot] + q * Q, Q), :],
            send_sem=ag_send.at[dirn, t - 1, i],
            recv_sem=ag_recv.at[dirn, t - 1, i],
            device_id=dev(d, targets[dirn]),
            device_id_type=MESH,
        )

    width = features // PIECES

    def pack_copy(dirn, n):
        cols = pl.ds(n * width, width)
        return pltpu.make_async_remote_copy(
            src_ref=pk.at[dirn, :, cols],
            dst_ref=tokbuf.at[pl.ds(place[packed[dirn]], CAP), cols],
            send_sem=ag_send.at[dirn, full[dirn], n],
            recv_sem=ag_recv.at[dirn, full[dirn], n],
            device_id=dev(d, targets[dirn]),
            device_id_type=MESH,
        )

    def ag_first(half):
        for q in range(2):
            for dirn in range(2):
                ag_copy(dirn, 1, half, q).start()

    def back_copy(dirn, n):
        cols = pl.ds(n * width, width)
        return pltpu.make_async_remote_copy(
            src_ref=pk_back.at[dirn, :, cols],
            dst_ref=pk_in.at[dirn, :, cols],
            send_sem=rs_send.at[dirn, 0, n],
            recv_sem=rs_recv.at[dirn, 0, n],
            device_id=dev(d, targets[1 - dirn]),
            device_id_type=MESH,
        )

    def rs_slots(dirn, t):
        return (nh + 1 - t, nh - t) if dirn == 0 else (nh + t, nh + 1 + t)

    def rs_copy(dirn, t, half, q):
        src_slot, dst_slot = rs_slots(dirn, t)
        i = half * 2 + q
        return pltpu.make_async_remote_copy(
            src_ref=rs.at[half, src_slot, pl.ds(q * Q, Q), :],
            dst_ref=rs.at[half, dst_slot, pl.ds(q * Q, Q), :],
            send_sem=rs_send.at[dirn, t - 1, i],
            recv_sem=rs_recv.at[dirn, t - 1, i],
            device_id=dev(d, targets[1 - dirn]),
            device_id_type=MESH,
        )

    def rs_hop(dirn, t, half, q):
        slot = rs_slots(dirn, t)[0]
        rows = pl.ds(q * Q, Q)
        total = contrib[pl.ds(place[half, slot] + q * Q, Q), :]
        if t > 2:
            rs_copy(dirn, t - 1, half, q).wait_recv()
            total = total + rs[half, slot, rows, :].astype(jnp.float32)
        rs[half, slot, rows, :] = total.astype(jnp.bfloat16)
        rs_copy(dirn, t, half, q).start()
        if t > 3:
            rs_copy(dirn, t - 2, half, q).wait_send()

    def rs_last(half, q):
        rows = pl.ds(q * Q, Q)
        rs_copy(0, nh, half, q).wait_recv()
        rs_copy(1, nh - 1, half, q).wait_recv()
        total = contrib[pl.ds(place[half, 0] + q * Q, Q), :]
        total = total + rs[half, 0, rows, :].astype(jnp.float32) + rs[half, nz, rows, :].astype(jnp.float32)
        out[pl.ds(half * HALF + q * Q, Q), :] = total.astype(jnp.bfloat16)

    sources = (gate, up, down)

    def whole(i, role):
        if i == 2:
            return wb.at[pl.ds(role * hdev, hdev), :]
        return (gb, ub)[i].at[role]

    def part(i, role, side):
        if i == 2:
            return wb.at[pl.ds(role * hdev + side * (hdev // 2), hdev // 2), :]
        return (gb, ub)[i].at[role, pl.ds(side * (features // 2), features // 2), :]

    def own_copy(i):
        return pltpu.make_async_copy(sources[i], whole(i, 0), own_sem.at[i])

    def piece(i, role, k):
        size = sources[i].shape[0] // 4
        if i == 2:
            return wb.at[pl.ds(role * hdev + k * size, size), :]
        return (gb, ub)[i].at[role, pl.ds(k * size, size), :]

    def sib_copy(i, k):
        size = sources[i].shape[0] // 4
        return pltpu.make_async_remote_copy(
            src_ref=sources[i].at[pl.ds(k * size, size), :], dst_ref=piece(i, 1, k),
            send_sem=sib_send.at[i, k], recv_sem=sib_recv.at[i, k],
            device_id=dev(d, sib), device_id_type=MESH)

    def x_copy(i, side):
        size = sources[i].shape[0] // 2
        return pltpu.make_async_remote_copy(
            src_ref=sources[i].at[pl.ds(side * size, size), :], dst_ref=part(i, 2, side),
            send_sem=x_send.at[i, side], recv_sem=x_recv.at[i, side],
            device_id=dev(d if side == 0 else d_other, xq), device_id_type=MESH)

    def fw_copy(i, k):
        return pltpu.make_async_remote_copy(
            src_ref=piece(i, 2, k), dst_ref=piece(i, 3, k),
            send_sem=fw_send.at[i, k], recv_sem=fw_recv.at[i, k],
            device_id=dev(d, sib), device_id_type=MESH)

    def forward(i, side):
        x_copy(i, side).wait_recv()
        for k in range(2):
            fw_copy(i, side * 2 + k).start()

    def arrive(i, role):
        if role == 0:
            own_copy(i).wait()
        for k in range(4):
            if role == 1:
                sib_copy(i, k).wait_recv()
            elif role == 3:
                fw_copy(i, k).wait_recv()

    def share_has(dirn, t):
        return t < nh or dirn == 0

    def share_copy(dirn, t):
        src_slot, dst_slot = (t - 1, t) if dirn == 0 else ((nz - t + 1) % nz, nz - t)
        return pltpu.make_async_remote_copy(
            src_ref=shr.at[src_slot], dst_ref=shr.at[dst_slot],
            send_sem=sh_send.at[dirn, t - 1], recv_sem=sh_recv.at[dirn, t - 1],
            device_id=dev(d, targets[dirn]), device_id_type=MESH)

    def make_shares():
        experts = lax.broadcasted_iota(jnp.int32, (nz, 64), 0)
        counts = jnp.zeros((nz, 64), jnp.float32)
        raw = jnp.zeros((nz, 64), jnp.float32)
        for k in range(ids.shape[0]):
            match = ids[k:k + 1, :] == experts
            counts = counts + jnp.where(match, 1.0, 0.0)
            raw = raw + jnp.where(match, rw[k:k + 1, :], 0.0)
        before = lax.broadcasted_iota(jnp.int32, (64, 64), 0) < lax.broadcasted_iota(jnp.int32, (64, 64), 1)
        places = jnp.dot(counts.astype(jnp.bfloat16), jnp.where(before, 1.0, 0.0).astype(jnp.bfloat16),
                         preferred_element_type=jnp.float32)
        shares = jnp.where((counts == 1.0) & (places < CAP), raw, 0.0)
        for k in range(nz // 8):
            shr[0, :, k * 64:(k + 1) * 64] = shares[k * 8:(k + 1) * 8, :]

    def take_shares(slots):
        lane = lax.broadcasted_iota(jnp.int32, (64, 128), 1)
        row = lax.broadcasted_iota(jnp.int32, (64, 128), 0)
        diag = lane == row + 64 * (z // 8)
        for slot in slots:
            mine = shr[slot, pl.ds(lax.rem(z, 8), 1), :]
            column = jnp.sum(jnp.where(diag, mine, 0.0), axis=1, keepdims=True)
            for half in range(2):
                shc[pl.ds(place[half, slot], HALF), :] = column[half * HALF:(half + 1) * HALF]

    def chosen(slot, expert):
        both = shr[slot, pl.ds(lax.rem(expert, 8), 1), :]
        share = jnp.where(expert >= 8, both[:, 64:], both[:, :64])
        kept = jnp.where(share > 0.0, 1.0, 0.0)
        before = lax.broadcasted_iota(jnp.int32, (64, 64), 0) < lax.broadcasted_iota(jnp.int32, (64, 64), 1)
        place_of = jnp.dot(jnp.broadcast_to(kept, (16, 64)).astype(jnp.bfloat16), jnp.where(before, 1.0, 0.0).astype(jnp.bfloat16),
                           preferred_element_type=jnp.float32)[:1]
        place_of = jnp.where(kept > 0.0, place_of, -1.0)
        slots = lax.broadcasted_iota(jnp.int32, (CAP, 64), 0).astype(jnp.float32)
        return share, place_of, jnp.where(slots == place_of, 1.0, 0.0)

    def prepare(dirn):
        share, place_of, pick = chosen(packer[dirn], next_plane[dirn])
        oh[dirn, :, :] = pick.astype(jnp.bfloat16)
        diag = lax.broadcasted_iota(jnp.int32, (64, 64), 0) == lax.broadcasted_iota(jnp.int32, (64, 64), 1)
        column = jnp.sum(jnp.where(diag, place_of, 0.0), axis=1, keepdims=True)
        slots = lax.broadcasted_iota(jnp.int32, (64, CAP), 1).astype(jnp.float32)
        oht[dirn, :, :] = jnp.where(slots == column, 1.0, 0.0).astype(jnp.bfloat16)

    def pack(dirn):
        for n in range(PIECES):
            cols = pl.ds(n * width, width)
            block = tokbuf[pl.ds(place[0, packer[dirn]], 2 * HALF), cols]
            pk[dirn, :, cols] = jnp.dot(oh[dirn], block, preferred_element_type=jnp.float32).astype(jnp.bfloat16)
            pack_copy(dirn, n).start()

    def packed_arrived(dirn):
        for n in range(PIECES):
            pack_copy(dirn, n).wait_recv()

    def take_packed_shares(dirn):
        share, place_of, pick = chosen(packed[dirn], z)
        shc[pl.ds(place[packed[dirn]], CAP), :] = jnp.sum(pick * share, axis=1, keepdims=True)

    def send_back(dirn, n):
        cols = pl.ds(n * width, width)
        pk_back[dirn, :, cols] = contrib[pl.ds(place[packed[dirn]], CAP), cols].astype(jnp.bfloat16)
        back_copy(dirn, n).start()

    def unpack(dirn):
        rows = pl.ds(place[0, packer[dirn]], 2 * HALF)
        for n in range(PIECES):
            back_copy(dirn, n).wait_recv()
            cols = pl.ds(n * width, width)
            contrib[rows, cols] = contrib[rows, cols] + jnp.dot(oht[dirn], pk_in[dirn, :, cols], preferred_element_type=jnp.float32)
        for half in range(2):
            for q in range(2):
                rs_hop(dirn, 2, half, q)

    def hidden(m, role):
        rows = pl.ds(*tiles[m])
        x = tokbuf[rows, :]
        g = jnp.dot(x, gb[role], preferred_element_type=jnp.float32)
        v = jnp.dot(x, ub[role], preferred_element_type=jnp.float32)
        hid[rows, role * hdev:(role + 1) * hdev] = (g / (1.0 + jnp.exp(-g)) * v).astype(jnp.bfloat16)

    def project(m, n):
        rows = pl.ds(*tiles[m])
        cols = slice(n * width, (n + 1) * width)
        acc = jnp.dot(hid[rows, :], wb[:, cols], preferred_element_type=jnp.float32)
        contrib[rows, cols] = acc * shc[rows, :]

    own_tokens = [
        pltpu.make_async_copy(tok.at[pl.ds(half * HALF, HALF), :], tokbuf.at[pl.ds(place[half, 0], HALF), :], own_sem.at[3 + half])
        for half in range(2)
    ]
    small = [pltpu.make_async_copy(ids_hbm, ids, in_sem.at[0]), pltpu.make_async_copy(rw_hbm, rw, in_sem.at[1])]
    for copy in small:
        copy.start()
    for i in range(3):
        own_copy(i).start()
    for copy in own_tokens:
        copy.start()
    for copy in small:
        copy.wait()
    make_shares()
    pl.semaphore_wait(barrier, len(peers))

    ag_first(0)
    for dirn in range(2):
        share_copy(dirn, 1).start()
    ag_first(1)
    for i in range(2):
        for side in range(2):
            x_copy(i, side).start()

    def spread(half, t, q):
        for dirn in range(2):
            if t <= full[dirn]:
                ag_copy(dirn, t, half, q).wait_recv()
            if t + 1 <= full[dirn]:
                ag_copy(dirn, t + 1, half, q).start()

    def spread_shares(t):
        for dirn in range(2):
            if share_has(dirn, t):
                share_copy(dirn, t).wait_recv()
            if t < nh and share_has(dirn, t + 1):
                share_copy(dirn, t + 1).start()

    copies, products = [], []

    def step(hop):
        for queue in (copies, products):
            if queue and queue[0][0] <= hop:
                call = queue.pop(0)
                call[1](*call[2:])

    def arrive_both(role):
        arrive(0, role)
        arrive(1, role)

    def own_arrived():
        for copy in own_tokens:
            copy.wait()
        arrive_both(0)

    def start_sib(i, k):
        sib_copy(i, k).start()

    def start_down():
        for side in range(2):
            x_copy(2, side).start()

    def arrive_down():
        for role in range(4):
            arrive(2, role)

    for k in range(4):
        for i in range(2):
            copies.append((1, start_sib, i, k))
    copies.append((2, start_down))
    for k in range(4):
        copies.append((3, start_sib, 2, k))
    for i in range(2):
        for side in range(2):
            copies.append((4.2, forward, i, side))
    for side in range(2):
        copies.append((6.3, forward, 2, side))

    products.append((4, own_arrived))
    products.append((4.1, arrive_both, 1))
    for role in range(2):
        for half in range(2):
            products.append((4.1 + half * 0.2, hidden, ("A0", "A1")[half], role))
    for half in range(2):
        products.append((5.2, hidden, ("A0", "A1")[half], 2))
    products.append((6, arrive_both, 3))
    for half in range(2):
        products.append((6, hidden, ("A0", "A1")[half], 3))
    for role in range(4):
        products.append((6.3, hidden, "B", role))
    products.append((6.3, take_shares, order[:nh + nh // 2]))

    for t in range(1, nh):
        for half in range(2):
            for q in range(2):
                spread(half, t, q)
                if half == 0 and q == 1:
                    spread_shares(t)
                    for dirn in range(2):
                        if t == full[dirn]:
                            prepare(dirn)
                for dirn in range(2):
                    if (t, half, q) == (full[dirn], 1, 1):
                        pack(dirn)
                step(t + 0.1 * (2 * half + q))
    while copies or products:
        step(nh)

    take_shares(late)
    take_packed_shares(1)
    arrive_down()
    packed_arrived(1)
    for role in range(4):
        hidden("C", role)
    for n in range(PIECES):
        project("C", n)
        send_back(1, n)
    spread_shares(nh)
    take_packed_shares(0)
    packed_arrived(0)
    for role in range(4):
        hidden("D", role)
    for n in range(PIECES):
        project("D", n)
        send_back(0, n)
    unpack(1)
    for n in range(PIECES):
        project("B", n)
    unpack(0)

    done = []
    for tt in range(1, nh + 1):
        for half in range(2):
            for q in range(2):
                for dirn in range(2):
                    if tt <= full[dirn]:
                        done.append(ag_copy(dirn, tt, half, q))
        for dirn in range(2):
            if share_has(dirn, tt):
                done.append(share_copy(dirn, tt))
    for dirn in range(2):
        for n in range(PIECES):
            done.append(pack_copy(dirn, n))
            done.append(back_copy(dirn, n))
    for i in range(3):
        for k in range(4):
            done.append(sib_copy(i, k))
            done.append(fw_copy(i, k))
        for side in range(2):
            done.append(x_copy(i, side))

    def sent(copies):
        for copy in copies:
            copy.wait_send()

    for half in range(2):
        for n in range(PIECES):
            products.append((2, project, ("A0", "A1")[half], n))
    for i in range(0, len(done), 8):
        products.append((4, sent, done[i:i + 8]))

    for t in range(3, nh + 1):
        for half in range(2):
            for q in range(2):
                if t < nh:
                    rs_hop(1, t, half, q)
                step(t)
                rs_hop(0, t, half, q)
    for half in range(2):
        for q in range(2):
            rs_last(half, q)
    while products:
        step(nh + 1)
    for half in range(2):
        for q in range(2):
            for dirn in range(2):
                for t in range(full[dirn], full[dirn] + 2):
                    rs_copy(dirn, t, half, q).wait_send()


def solution(mesh):
    nz = mesh.shape["expert"] // 4
    nh = nz // 2

    def on_device(tokens, gate, up, down, ids, rw):
        rows, features = tokens.shape
        hdev = gate.shape[1]
        dma = pltpu.SemaphoreType.DMA
        flops = 2 * rows * nz * features * 4 * hdev * 3
        return pl.pallas_call(
            functools.partial(kernel, nz),
            out_shape=pltpu.VMEM((rows, features), jnp.bfloat16),
            in_specs=[pl.BlockSpec(memory_space=pl.ANY)] * 6,
            out_specs=pl.BlockSpec(memory_space=pltpu.VMEM),
            scratch_shapes=[
                pltpu.VMEM((nz * rows, features), jnp.bfloat16),
                pltpu.VMEM((2, nz + 1, HALF, features), jnp.bfloat16),
                pltpu.VMEM((nz * rows, features), jnp.float32),
                pltpu.VMEM((nz * rows, 4 * hdev), jnp.bfloat16),
                pltpu.VMEM((4, features, hdev), jnp.bfloat16),
                pltpu.VMEM((4, features, hdev), jnp.bfloat16),
                pltpu.VMEM((4 * hdev, features), jnp.bfloat16),
                pltpu.VMEM((nz, 8, 128), jnp.float32),
                pltpu.VMEM((nz * rows, 1), jnp.float32),
                pltpu.VMEM((ids.shape[1], rows), jnp.int32),
                pltpu.VMEM((ids.shape[1], rows), jnp.float32),
                pltpu.VMEM((2, CAP, features), jnp.bfloat16),
                pltpu.VMEM((2, CAP, features), jnp.bfloat16),
                pltpu.VMEM((2, CAP, features), jnp.bfloat16),
                pltpu.VMEM((2, CAP, rows), jnp.bfloat16),
                pltpu.VMEM((2, rows, CAP), jnp.bfloat16),
                dma((2, nh, 4)),
                dma((2, nh, 4)),
                dma((2, nh, 4)),
                dma((2, nh, 4)),
                dma((5,)),
                dma((3, 4)),
                dma((3, 4)),
                dma((3, 2)),
                dma((3, 2)),
                dma((3, 4)),
                dma((3, 4)),
                dma((2, nh)),
                dma((2, nh)),
                dma((2,)),
            ],
            compiler_params=pltpu.CompilerParams(
                collective_id=0, has_side_effects=True, vmem_limit_bytes=56 * 1024 * 1024
            ),
            cost_estimate=pl.CostEstimate(flops=flops, bytes_accessed=4 * 1024 * 1024, transcendentals=0),
        )(tokens, gate, up, down, ids.T, rw.T)

    return jax.shard_map(
        on_device,
        mesh=mesh,
        in_specs=(
            P(("dp", "expert"), None),
            P(None, "expert"),
            P(None, "expert"),
            P("expert", None),
            P(("dp", "expert"), None),
            P(("dp", "expert"), None),
        ),
        out_specs=P(("dp", "expert"), None),
        check_vma=False,
    )
```
